512 devices in a mesh: seq: 64 (over x, z, core), mp: 8 (over y).
Axes of the slice: x: 4, y: 8, z: 8, core: 2. Of those that a mesh axis runs over, the one named last changes fastest.
Arguments:
- queries: bfloat16 [32768, 2048], P('seq', 'mp'), may hold values from -30 to 30
- stretch_kv: bfloat16 [32768, 1792], P(('seq', 'mp')), may hold values from -5 to 5
- pool: bfloat16 [512, 64, 896], P('seq', 'mp'), may hold values from -20 to 20
- neighbour_owner: int32 [512, 2], replicated, may hold values from 0 to 63, all different within a row; in each aligned block of 8 rows (0 to 7, 8 to 15, ...) at most 2 rows name the same one
- neighbour_slot: int32 [512, 2], replicated, may hold values from 0 to 7
- enc_query_weight: bfloat16 [896, 896], P('mp'), may hold values from -0.1875 to 0.1875
- dec_kv_weight: bfloat16 [896, 2, 2048], P(None, None, 'mp'), may hold values from -0.1875 to 0.1875
- out_cotangent: bfloat16 [32768, 2048], P('seq', 'mp'), may hold values from -5 to 5
Outputs:
- attended: bfloat16 [32768, 2048], P('seq', 'mp')
- grad_queries: bfloat16 [32768, 2048], P('seq', 'mp')
- grad_pool: float32 [512, 64, 896], P('seq', 'mp')
The draws below stay inside these ranges and needn't reach their ends.
Inputs may be any that keep to these rules, and one draw needn't show every extreme that they name: `neighbour_owner`: the 8 stretches of one index of seq name one owner at most 2 times, a bound that some block reaches; the 2 neighbours of a stretch have different owners.
All inputs are finite; a program needn't handle non-finite values.
Results may differ from the reference program's by a relative error of at most 0.034.
Values may be sent and summed in bfloat16 or wider, within the bound.
No kernel may reach another device: no remote copies, remote signals or barrier semaphores. Data moves between devices by JAX's collectives and lax.ppermute only.
A program may use at most 64 MiB of HBM per device.

```python
import math
import jax
import jax.numpy as jnp
import numpy as np
from jax import lax

STRETCH_DEV = 8
STRETCH_LEN = 64
NB_LEN = 64
NEIGHBOURS = 2
CAP = 2
POOL_DEV = 8
D_ENC = 896
HEAD_DIM = 128
DEC_HEADS = 16
TOKENS = 32768
STRETCHES = 512
POOL = 512
DEC_WIDTH = 2048
N_SEQ = 64
N_MP = 8


def draw_queries(key, part):
    key = jax.random.fold_in(key, 11)
    first = jax.random.fold_in(key, 0)
    base = jax.random.normal(first, (TOKENS, DEC_WIDTH), jnp.float32)
    values = jnp.clip(base, -5.0, 5.0)
    return values.astype(jnp.bfloat16)


def draw_pool(key, part):
    key = jax.random.fold_in(key, 23)
    first = jax.random.fold_in(key, 0)
    base = jax.random.normal(first, (POOL, NB_LEN, D_ENC), jnp.float32)
    values = jnp.clip(base, -5.0, 5.0)
    return values.astype(jnp.bfloat16)


def place_ends(array, key, smallest, top_value):
    spot = [jax.random.randint(jax.random.fold_in(key, axis), (), 0, length) for axis, length in enumerate(array.shape)]
    longest = array.shape.index(max(array.shape))
    neighbour = spot[:longest] + [(spot[longest] + 1) % array.shape[longest]] + spot[longest + 1:]
    return array.at[tuple(spot)].set(smallest).at[tuple(neighbour)].set(top_value)


def block_levels(rng, extent, cuts, least, top_value):
    def one(axis_at, shards_of):
        draws = jax.random.uniform(jax.random.fold_in(jax.random.fold_in(rng, 6), axis_at), (shards_of,), jnp.float32, least / len(cuts), top_value / len(cuts))
        return jnp.repeat(jnp.exp(draws), extent[axis_at] // shards_of).reshape((-1,) + (1,) * (len(extent) - axis_at - 1))

    factor_of = one(*cuts[0])
    for cut in cuts[1:]:
        factor_of = factor_of * one(*cut)
    return factor_of


def routed_block(rng, own, number, rows, amount, top, bound, lean):
    ranking = jax.random.permutation(rng, amount)
    crowded, common = shares(amount, rows * top, bound, lean, True), shares(amount, rows * top, bound, lean, False)
    places = jnp.arange(amount)

    def named(lengths, turn):
        used = int((lengths > 0).sum())
        fixed = max(1, used // 4)
        shifted = fixed + (places - fixed + turn * (used - fixed)) % max(1, amount - fixed)
        return jnp.zeros((amount,), jnp.int32).at[ranking[jnp.where(places < fixed, places, shifted)]].set(jnp.asarray(lengths, jnp.int32))

    lengths = jnp.where(number % 4 == 0, named(crowded, number // 4), named(common, number - number // 4 - 1))
    mixed = jax.random.permutation(jax.random.fold_in(own, 3), amount)
    donor, receiver = mixed[0:amount // 2 * 2:2], mixed[1:amount // 2 * 2:2]
    margin = jnp.minimum(lengths[donor] - 1, bound - lengths[receiver]) // 2
    margin = jnp.where((donor == ranking[0]) | (receiver == ranking[0]) | (lengths[receiver] == 0), 0, jnp.maximum(margin, 0))
    shifted = jax.random.randint(jax.random.fold_in(own, 4), (amount // 2,), 0, 1 << 20) % (margin + 1)
    lengths = lengths.at[donor].add(-shifted).at[receiver].add(shifted)
    members = jnp.searchsorted(jnp.cumsum(lengths), jnp.arange(rows * top), side="right").astype(jnp.int32)
    listing = members.reshape(top, rows).T
    listing = listing[jax.random.permutation(jax.random.fold_in(own, 1), rows)]
    turn = jax.random.randint(jax.random.fold_in(own, 2), (rows, 1), 0, top)
    return jnp.take_along_axis(listing, (jnp.arange(top)[None, :] + turn) % top, axis=1)


def shares(count, total, most, skew, full):
    loads = [(1 << 20) // math.isqrt(rank ** skew) + 1 for rank in range(1, count + 1)]
    largest = most if full else min(most, max(-(-total // count), total * loads[0] // sum(loads)))
    least = 1 if total - largest >= count - 1 else 0
    holding, spare = [largest] + [least] * (count - 1), total - largest - least * (count - 1)
    while spare > 0:
        candidates = [i for i in range(1, count) if holding[i] < largest] or [i for i in range(1, count) if holding[i] < most]
        mass, left = sum([loads[i] for i in candidates]), spare
        for i in candidates:
            more = min(most - holding[i], max(1, left * loads[i] // mass), spare)
            holding[i] = holding[i] + more
            spare = spare - more
    return np.array(holding)


def scatter_about(rng, dims, deviation, limit, cuts=(), held_as=jnp.bfloat16):
    result = deviation * jax.random.normal(rng, dims, jnp.float32)
    if cuts:
        result = result * block_levels(rng, dims, cuts, -0.22, 0.18)
    return jnp.clip(result, -limit, limit).astype(held_as)


def setup_inputs(seed: int = 0) -> dict:
    streams_of = jax.random.split(jax.random.key(seed), 9)
    queries = draw_queries(jax.random.fold_in(streams_of[8], 71), 0)
    stretch_kv = scatter_about(streams_of[1], (TOKENS, 2 * D_ENC), 1.0, 5.0, ((0, 512),))
    pool = draw_pool(jax.random.fold_in(streams_of[8], 71), 0)
    neighbour_owner_keys = jax.random.split(jax.random.fold_in(streams_of[3], 1), STRETCHES // STRETCH_DEV)
    neighbour_owner_turns = jax.random.permutation(jax.random.fold_in(streams_of[3], 3), STRETCHES // STRETCH_DEV)
    neighbour_owner = jax.vmap(lambda own, number: routed_block(jax.random.fold_in(streams_of[3], 2), own, number, STRETCH_DEV, N_SEQ, NEIGHBOURS, CAP, 2))(neighbour_owner_keys, neighbour_owner_turns).reshape((STRETCHES, NEIGHBOURS))
    neighbour_slot = place_ends(jax.random.randint(streams_of[4], (STRETCHES, NEIGHBOURS), 0, POOL_DEV), jax.random.fold_in(streams_of[4], 1), 0, POOL_DEV - 1).astype(jnp.int32)
    enc_query_weight = scatter_about(streams_of[5], (D_ENC, D_ENC), D_ENC ** -0.5, 0.1875, ((0, 8),))
    dec_kv_weight = scatter_about(streams_of[6], (D_ENC, 2, DEC_WIDTH), D_ENC ** -0.5, 0.1875, ((2, 8),))
    out_cotangent = scatter_about(streams_of[7], (TOKENS, DEC_WIDTH), 1.0, 5.0, ((0, 64), (1, 8)))
    return {"queries": queries, "stretch_kv": stretch_kv, "pool": pool, "neighbour_owner": neighbour_owner, "neighbour_slot": neighbour_slot, "enc_query_weight": enc_query_weight, "dec_kv_weight": dec_kv_weight, "out_cotangent": out_cotangent}


def encoder_parts(rows, context, weight):
    count, pair, span, width = rows.shape
    heads = width // HEAD_DIM
    query = jnp.dot(rows.reshape(-1, width), weight, preferred_element_type=jnp.float32).astype(jnp.bfloat16)
    query = query.reshape(count, pair, span, heads, HEAD_DIM)
    keys = context[:, :, :width].reshape(count, -1, heads, HEAD_DIM)
    values = context[:, :, width:].reshape(count, -1, heads, HEAD_DIM)
    scores = jnp.einsum("cnthd,cshd->cnhts", query.astype(jnp.float32), keys.astype(jnp.float32)) * HEAD_DIM ** -0.5
    weights = jax.nn.softmax(scores, axis=-1)
    return weights, keys, values


def encode(rows, context, weight):
    weights, keys, values = encoder_parts(rows, context, weight)
    mixed = jnp.einsum("cnhts,cshd->cnthd", weights.astype(jnp.bfloat16).astype(jnp.float32), values.astype(jnp.float32))
    return (rows.astype(jnp.float32) + mixed.reshape(rows.shape)).astype(jnp.bfloat16)


def encode_back(rows, context, weight, grad_out):
    weights, keys, values = encoder_parts(rows, context, weight)
    count, pair, span, width = rows.shape
    heads = width // HEAD_DIM
    grad_heads = grad_out.reshape(count, pair, span, heads, HEAD_DIM).astype(jnp.float32)
    grad_w = jnp.einsum("cnthd,cshd->cnhts", grad_heads, values.astype(jnp.float32))
    grad_s = (weights * (grad_w - jnp.sum(grad_w * weights, axis=-1, keepdims=True))).astype(jnp.bfloat16)
    grad_q = (jnp.einsum("cnhts,cshd->cnthd", grad_s.astype(jnp.float32), keys.astype(jnp.float32)) * HEAD_DIM ** -0.5).astype(jnp.bfloat16)
    back = jnp.dot(grad_q.reshape(-1, width).astype(jnp.float32), weight.astype(jnp.float32).T)
    return (grad_out.astype(jnp.float32) + back.reshape(rows.shape)).astype(jnp.bfloat16)


def reference(queries, stretch_kv, pool, neighbour_owner, neighbour_slot, enc_query_weight, dec_kv_weight, out_cotangent):
    index = (neighbour_owner * POOL_DEV + neighbour_slot).astype(jnp.int32)
    scale = HEAD_DIM ** -0.5
    weight_groups = dec_kv_weight.astype(jnp.float32).reshape(D_ENC, 2, N_MP, DEC_WIDTH // N_MP)

    def block(items):
        query, context, where, cot = items
        rows = pool[where]
        encoded = encode(rows, context, enc_query_weight)
        projected = jnp.einsum("cnte,ekf->cntkf", encoded.astype(jnp.float32), dec_kv_weight.astype(jnp.float32)).astype(jnp.bfloat16)
        keys = projected[:, :, :, 0, :].reshape(STRETCH_DEV, NEIGHBOURS * NB_LEN, DEC_HEADS, HEAD_DIM).astype(jnp.float32)
        values = projected[:, :, :, 1, :].reshape(STRETCH_DEV, NEIGHBOURS * NB_LEN, DEC_HEADS, HEAD_DIM).astype(jnp.float32)
        qf = query.astype(jnp.float32)
        scores = jnp.einsum("cqhd,ckhd->chqk", qf, keys) * scale
        weights = jax.nn.softmax(scores, axis=-1)
        wb = weights.astype(jnp.bfloat16).astype(jnp.float32)
        out = jnp.einsum("chqk,ckhd->cqhd", wb, values).astype(jnp.bfloat16)
        gf = cot.astype(jnp.float32)
        grad_v = jnp.einsum("chqk,cqhd->ckhd", wb, gf).astype(jnp.bfloat16)
        grad_w = jnp.einsum("cqhd,ckhd->chqk", gf, values)
        grad_s = (weights * (grad_w - jnp.sum(grad_w * weights, axis=-1, keepdims=True))).astype(jnp.bfloat16).astype(jnp.float32)
        grad_q = (jnp.einsum("chqk,ckhd->cqhd", grad_s, keys) * scale).astype(jnp.bfloat16)
        grad_k = (jnp.einsum("chqk,cqhd->ckhd", grad_s, qf) * scale).astype(jnp.bfloat16)
        grad_kv = jnp.stack((grad_k.reshape(STRETCH_DEV, NEIGHBOURS, NB_LEN, DEC_WIDTH), grad_v.reshape(STRETCH_DEV, NEIGHBOURS, NB_LEN, DEC_WIDTH)), axis=3)
        grad_kv = grad_kv.astype(jnp.float32).reshape(STRETCH_DEV, NEIGHBOURS, NB_LEN, 2, N_MP, DEC_WIDTH // N_MP)
        terms = jnp.einsum("cntkmf,ekmf->mcnte", grad_kv, weight_groups).astype(jnp.bfloat16).astype(jnp.float32)
        grad_encoded = jnp.sum(terms, axis=0).astype(jnp.bfloat16)
        grad_rows = encode_back(rows, context, enc_query_weight, grad_encoded)
        return out, grad_q, grad_rows

    items = (queries.reshape(N_SEQ, STRETCH_DEV, STRETCH_LEN, DEC_HEADS, HEAD_DIM),
             stretch_kv.reshape(N_SEQ, STRETCH_DEV, STRETCH_LEN, 2 * D_ENC),
             index.reshape(N_SEQ, STRETCH_DEV, NEIGHBOURS),
             out_cotangent.reshape(N_SEQ, STRETCH_DEV, STRETCH_LEN, DEC_HEADS, HEAD_DIM))
    out, grad_q, grad_rows = lax.map(block, items)
    grad_pool = jnp.zeros((POOL, NB_LEN, D_ENC), jnp.float32)
    grad_pool = grad_pool.at[index.reshape(-1)].add(grad_rows.reshape(-1, NB_LEN, D_ENC).astype(jnp.float32))
    return out.reshape(TOKENS, DEC_WIDTH), grad_q.reshape(TOKENS, DEC_WIDTH), grad_pool
```

```python
import jax
import jax.numpy as jnp
from jax import lax
from jax.experimental import pallas as pl
from jax.experimental.pallas import tpu as pltpu
from jax.sharding import Mesh
from jax.sharding import PartitionSpec as P

HEAD_DIM = 128
SCALE = HEAD_DIM ** (-0.5)
SEQ = ("x", "z", "core")
NX, NZ, NC, NM = 4, 8, 2, 8
REQ = 16
SLOTS = 8
STRETCH = 64
SPAN = 8
WIDTH = 896
ENC_HEADS = 7
KV = 2 * HEAD_DIM
ENC_ROWS = 112
PACK = WIDTH + 2 * ENC_ROWS


def dot(a, b, dims):
    return lax.dot_general(a, b, ((dims[0], dims[1]), ((), ())), preferred_element_type=jnp.float32)


def softmax(scores):
    top = jnp.max(scores, axis=-1, keepdims=True)
    e = jnp.exp(scores - top)
    return e / jnp.sum(e, axis=-1, keepdims=True)


def softmax_back(weights, grad):
    return weights * (grad - jnp.sum(grad * weights, axis=-1, keepdims=True))


def stretch_kernel(
    core_ref,
    rows_ref,
    kv_ref,
    qg_ref,
    mine_ref,
    other_ref,
    out_ref,
    grad_ref,
    enc_w,
    dec_w,
    encoded_ref,
    heads_ref,
    probs_ref,
    total_ref,
    enc_sem,
    dec_sem,
):
    core = core_ref[0]
    enc_copies = []
    for source in range(2):
        ref = mine_ref if source == 0 else other_ref
        for m in range(NM):
            for pair in range(2):
                enc_copies.append(
                    pltpu.make_async_copy(
                        ref.at[m, pl.ds(WIDTH + pair * ENC_ROWS, ENC_ROWS), :],
                        enc_w.at[source, pl.ds(m * ENC_ROWS, ENC_ROWS), pl.ds(pair * KV, KV)],
                        enc_sem.at[source, m, pair],
                    )
                )
    for copy in enc_copies:
        copy.start()
    dec_copies = []
    for m in range(NM):
        pair = []
        for source in range(2):
            ref = mine_ref if source == 0 else other_ref
            head = core if source == 0 else 1 - core
            pair.append(
                pltpu.make_async_copy(
                    ref.at[m, pl.ds(0, WIDTH), :], dec_w.at[m, head], dec_sem.at[m, source]
                )
            )
        dec_copies.append(pair)
        for copy in pair:
            copy.start()
    for copy in enc_copies:
        copy.wait()

    rows = rows_ref[...]
    low = enc_w[core]
    high = enc_w[1 - core]
    weight = jnp.concatenate([low, high[:, 128:]], axis=1)
    query = dot(rows, weight, ((1,), (0,))).astype(jnp.bfloat16)
    for h in range(ENC_HEADS):
        cols = slice(h * HEAD_DIM, (h + 1) * HEAD_DIM)
        keys = kv_ref[:, cols]
        values = kv_ref[:, WIDTH + h * HEAD_DIM : WIDTH + (h + 1) * HEAD_DIM]
        weights = softmax(dot(query[:, cols], keys, ((1,), (1,))) * SCALE)
        probs_ref[h] = weights
        mixed = dot(weights.astype(jnp.bfloat16), values, ((1,), (0,)))
        encoded_ref[:, cols] = (rows[:, cols].astype(jnp.float32) + mixed).astype(jnp.bfloat16)
    encoded = encoded_ref[...]

    for m in range(NM):
        for copy in dec_copies[m]:
            copy.wait()
        for h in range(2):
            cols = slice(h * HEAD_DIM, (h + 1) * HEAD_DIM)
            both = dot(encoded, dec_w[m, h], ((1,), (0,))).astype(jnp.bfloat16)
            keys, values = both[:, :HEAD_DIM], both[:, HEAD_DIM:]
            q = qg_ref[m, :STRETCH, cols]
            g = qg_ref[m, STRETCH:, cols]
            weights = softmax(dot(q, keys, ((1,), (1,))) * SCALE)
            low_w = weights.astype(jnp.bfloat16)
            out_ref[m, :STRETCH, cols] = dot(low_w, values, ((1,), (0,))).astype(jnp.bfloat16)
            grad_s = softmax_back(weights, dot(g, values, ((1,), (1,)))).astype(jnp.bfloat16)
            out_ref[m, STRETCH:, cols] = (dot(grad_s, keys, ((1,), (0,))) * SCALE).astype(
                jnp.bfloat16
            )
            grad_v = dot(low_w, g, ((0,), (0,))).astype(jnp.bfloat16)
            grad_k = (dot(grad_s, q, ((0,), (0,))) * SCALE).astype(jnp.bfloat16)
            term = dot(jnp.concatenate([grad_k, grad_v], axis=1), dec_w[m, h], ((1,), (1,)))
            if m == 0 and h == 0:
                total_ref[...] = term
            else:
                total_ref[...] += term

    grad_encoded = total_ref[...].astype(jnp.bfloat16)
    for h in range(ENC_HEADS):
        cols = slice(h * HEAD_DIM, (h + 1) * HEAD_DIM)
        keys = kv_ref[:, cols]
        values = kv_ref[:, WIDTH + h * HEAD_DIM : WIDTH + (h + 1) * HEAD_DIM]
        grad_w = dot(grad_encoded[:, cols], values, ((1,), (1,)))
        grad_s = softmax_back(probs_ref[h], grad_w).astype(jnp.bfloat16)
        heads_ref[:, cols] = (dot(grad_s, keys, ((1,), (0,))) * SCALE).astype(jnp.bfloat16)
    back = dot(heads_ref[...], weight, ((1,), (1,)))
    grad_ref[...] = (grad_encoded.astype(jnp.float32) + back).astype(jnp.bfloat16)


def stretch_call(core, rows, kv, qg, mine, other):
    vmem = pl.BlockSpec(memory_space=pltpu.VMEM)
    hbm = pl.BlockSpec(memory_space=pl.ANY)
    return pl.pallas_call(
        stretch_kernel,
        out_shape=(
            jax.ShapeDtypeStruct((NM, 2 * STRETCH, KV), jnp.bfloat16),
            jax.ShapeDtypeStruct((2 * STRETCH, WIDTH), jnp.bfloat16),
        ),
        in_specs=[pl.BlockSpec(memory_space=pltpu.SMEM), vmem, vmem, vmem, hbm, hbm],
        out_specs=(vmem, vmem),
        scratch_shapes=[
            pltpu.VMEM((2, WIDTH, 2 * KV), jnp.bfloat16),
            pltpu.VMEM((NM, 2, WIDTH, KV), jnp.bfloat16),
            pltpu.VMEM((2 * STRETCH, WIDTH), jnp.bfloat16),
            pltpu.VMEM((2 * STRETCH, WIDTH), jnp.bfloat16),
            pltpu.VMEM((ENC_HEADS, 2 * STRETCH, STRETCH), jnp.float32),
            pltpu.VMEM((2 * STRETCH, WIDTH), jnp.float32),
            pltpu.SemaphoreType.DMA((2, NM, 2)),
            pltpu.SemaphoreType.DMA((NM, 2)),
        ],
        compiler_params=pltpu.CompilerParams(vmem_limit_bytes=24 * 1024 * 1024),
        cost_estimate=pl.CostEstimate(
            flops=7_000_000_000, bytes_accessed=11_000_000, transcendentals=200_000
        ),
        name="stretch",
    )(core, rows, kv, qg, mine, other)


def place_kernel(place_ref, mine_ref, other_ref, out_ref, total_ref):
    total_ref[...] = jnp.zeros_like(total_ref)
    for source in range(2):
        ref = mine_ref if source == 0 else other_ref

        def add(i, carry, ref=ref, source=source):
            at = place_ref[source, i]
            total_ref[at] += ref[i].astype(jnp.float32)
            return carry

        lax.fori_loop(0, NX * REQ, add, 0, unroll=4)
    out_ref[...] = total_ref[: NZ * SLOTS].astype(jnp.bfloat16)


def place_call(place, mine, other):
    vmem = pl.BlockSpec(memory_space=pltpu.VMEM)
    return pl.pallas_call(
        place_kernel,
        out_shape=jax.ShapeDtypeStruct((NZ * SLOTS, SPAN, WIDTH), jnp.bfloat16),
        in_specs=[pl.BlockSpec(memory_space=pltpu.SMEM), vmem, vmem],
        out_specs=vmem,
        scratch_shapes=[pltpu.VMEM((NZ * SLOTS + 1, SPAN, WIDTH), jnp.float32)],
        compiler_params=pltpu.CompilerParams(vmem_limit_bytes=8 * 1024 * 1024),
        cost_estimate=pl.CostEstimate(
            flops=1_000_000, bytes_accessed=3_000_000, transcendentals=0
        ),
        name="place",
    )(place, mine, other)


def hops(k):
    index = [(z, core) for z in range(NZ) for core in range(NC)]
    return [
        (z * NC + core, (z + (k if core == 0 else -k)) % NZ * NC + core) for z, core in index
    ]


def shards(queries, stretch_kv, pool, owner, slot, enc_weight, dec_weight, cotangent):
    x, z, core = lax.axis_index("x"), lax.axis_index("z"), lax.axis_index("core")
    swap = [(0, 1), (1, 0)]

    own = lax.dynamic_slice_in_dim(dec_weight, core * HEAD_DIM, HEAD_DIM, axis=2)
    own = own.reshape(WIDTH, KV)
    enc_own = lax.dynamic_slice_in_dim(enc_weight, core * 384, 2 * KV, axis=1)
    packed = jnp.concatenate([own, enc_own[:, :KV], enc_own[:, KV:]], axis=0)
    mine = lax.all_gather(packed, "mp", axis=0, tiled=False)

    qg = jnp.concatenate(
        [queries.reshape(NM, STRETCH, KV), cotangent.reshape(NM, STRETCH, KV)], axis=1
    )

    owner = owner.reshape(NX, NZ, NC, REQ)
    slot = slot.reshape(NX, NZ, NC, REQ)
    owner_core = owner % NC
    owner_z = (owner // NC) % NZ
    owner_x = owner // (NC * NZ)
    row = owner_z * SLOTS + slot
    ahead = (owner_z - z) % NZ
    own_core = owner_core == core
    direct = jnp.where(core == 0, ahead > 4, ahead < 4)
    far = jnp.minimum(ahead, NZ - ahead)
    stored_row = slot + jnp.where(
        far == 0,
        jnp.where(own_core, 0, SLOTS),
        jnp.where(
            far == 4,
            jnp.where(own_core, 64, 120),
            far * 2 * SLOTS
            + jnp.where(direct, 0, 56)
            + jnp.where(own_core == direct, 0, SLOTS),
        ),
    )

    def of_column(values, which):
        return lax.dynamic_slice(values, (0, z, which, 0), (NX, 1, 1, REQ)).reshape(NX * REQ)

    beside = lax.ppermute(pool, "core", swap)
    chip = jnp.concatenate([pool, beside], axis=0)
    chip, qg = lax.optimization_barrier((chip, qg))
    qg = lax.all_to_all(qg, "mp", split_axis=0, concat_axis=0, tiled=True)
    came = [lax.ppermute(chip, ("z", "core"), hops(k)) for k in range(1, 4)]
    came.append(lax.ppermute(pool, ("z", "core"), hops(4)))
    swapped = [lax.ppermute(part, "core", swap) for part in came]
    stored = jnp.concatenate([chip, *came, *swapped], axis=0)
    ask = of_column(stored_row, core)
    chosen = jnp.take(stored, ask, axis=0, mode="clip")
    chosen, qg = lax.optimization_barrier((chosen, qg))
    arrived = lax.all_to_all(chosen, "x", split_axis=0, concat_axis=0, tiled=True)
    my_x = lax.dynamic_slice(owner_x, (x, z, core, 0), (1, 1, 1, REQ)).reshape(REQ)
    rows = jnp.take(arrived, my_x * REQ + jnp.arange(REQ), axis=0, mode="clip")
    _, mine = lax.optimization_barrier((rows, mine))
    other = lax.ppermute(mine, "core", swap)
    rows = lax.all_to_all(rows, "mp", split_axis=0, concat_axis=0, tiled=True)
    rows = rows.reshape(2 * STRETCH, WIDTH)

    out, grad_rows = stretch_call(
        core.reshape(1).astype(jnp.int32), rows, stretch_kv, qg, mine, other
    )

    grad_rows = grad_rows.reshape(REQ, SPAN, WIDTH)
    grad_rows = lax.all_to_all(grad_rows, "mp", split_axis=0, concat_axis=0, tiled=True)
    every = lax.all_gather(grad_rows, "x", axis=0, tiled=True)
    every_beside = lax.ppermute(every, "core", swap)

    def places(which):
        here = (of_column(owner_x, which) == x) & (of_column(owner_core, which) == core)
        return jnp.where(here, of_column(row, which), NZ * SLOTS)

    place = jnp.stack([places(core), places(1 - core)]).astype(jnp.int32)
    partial = place_call(place, every, every_beside)
    out = lax.all_to_all(out, "mp", split_axis=0, concat_axis=0, tiled=True)
    grad_pool = lax.psum_scatter(partial, "z", scatter_dimension=0, tiled=True)
    grad_pool = grad_pool.astype(jnp.float32)
    attended = out[:, :STRETCH].reshape(NM * STRETCH, KV)
    grad_queries = out[:, STRETCH:].reshape(NM * STRETCH, KV)
    return attended, grad_queries, grad_pool


def solution(mesh):
    split = Mesh(mesh.devices.reshape(NX, NZ, NC, NM), ("x", "z", "core", "mp"))
    in_specs = (
        P(SEQ, "mp"),
        P(SEQ + ("mp",), None),
        P(SEQ, "mp", None),
        P(),
        P(),
        P("mp", None),
        P(None, None, "mp"),
        P(SEQ, "mp"),
    )
    out_specs = (P(SEQ, "mp"), P(SEQ, "mp"), P(SEQ, "mp", None))
    return jax.shard_map(shards, mesh=split, in_specs=in_specs, out_specs=out_specs, check_vma=False)
```

```python
import jax
import jax.numpy as jnp
from jax import lax
from jax.experimental import pallas as pl
from jax.experimental.pallas import tpu as pltpu
from jax.sharding import Mesh
from jax.sharding import PartitionSpec as P

HEAD_DIM = 128
SCALE = HEAD_DIM ** (-0.5)
SEQ = ("x", "z", "core")
NX, NZ, NC, NM = 4, 8, 2, 8
REQ = 16
SLOTS = 8
STRETCH = 64
SPAN = 8
WIDTH = 896
ENC_HEADS = 7
KV = 2 * HEAD_DIM
ENC_ROWS = 112
NONE = NZ * SLOTS


def dot(a, b, dims):
    return lax.dot_general(a, b, ((dims[0], dims[1]), ((), ())), preferred_element_type=jnp.float32)


def softmax(scores):
    top = jnp.max(scores, axis=-1, keepdims=True)
    e = jnp.exp(scores - top)
    return e * (1.0 / jnp.sum(e, axis=-1, keepdims=True))


def softmax_back(weights, grad):
    return weights * (grad - jnp.sum(grad * weights, axis=-1, keepdims=True))


def stretch_kernel(
    rows_ref,
    kv_ref,
    qg_ref,
    packed_ref,
    out_ref,
    grad_ref,
    enc_w,
    dec_w,
    encoded_ref,
    heads_ref,
    probs_ref,
    total_ref,
    enc_sem,
    dec_sem,
):
    enc_copies = []
    for m in range(NM):
        for part, (core, pair, skip, column) in enumerate(
            ((0, 0, 0, 0), (0, 1, 0, 256), (1, 0, 128, 512), (1, 1, 0, 640))
        ):
            enc_copies.append(
                pltpu.make_async_copy(
                    packed_ref.at[
                        core * NM + m,
                        pl.ds(WIDTH + pair * ENC_ROWS, ENC_ROWS),
                        pl.ds(skip, KV - skip),
                    ],
                    enc_w.at[pl.ds(m * ENC_ROWS, ENC_ROWS), pl.ds(column, KV - skip)],
                    enc_sem.at[m, part],
                )
            )
    for copy in enc_copies:
        copy.start()
    dec_copies = []
    for m in range(NM):
        group = []
        for core in range(NC):
            for kind in range(2):
                group.append(
                    pltpu.make_async_copy(
                        packed_ref.at[
                            core * NM + m, pl.ds(0, WIDTH), pl.ds(kind * HEAD_DIM, HEAD_DIM)
                        ],
                        dec_w.at[m, :, pl.ds(kind * KV + core * HEAD_DIM, HEAD_DIM)],
                        dec_sem.at[m, core, kind],
                    )
                )
        dec_copies.append(group)
        for copy in group:
            copy.start()
    for copy in enc_copies:
        copy.wait()

    rows = rows_ref[...]
    query = dot(rows, enc_w[...], ((1,), (0,))).astype(jnp.bfloat16)
    for h in range(ENC_HEADS):
        cols = slice(h * HEAD_DIM, (h + 1) * HEAD_DIM)
        keys = kv_ref[:, cols]
        values = kv_ref[:, WIDTH + h * HEAD_DIM : WIDTH + (h + 1) * HEAD_DIM]
        weights = softmax(dot(query[:, cols], keys, ((1,), (1,))) * SCALE)
        probs_ref[h] = weights
        mixed = dot(weights.astype(jnp.bfloat16), values, ((1,), (0,)))
        encoded_ref[:, cols] = (rows[:, cols].astype(jnp.float32) + mixed).astype(jnp.bfloat16)
    encoded = encoded_ref[...]

    left = lax.broadcasted_iota(jnp.int32, (STRETCH, KV), 1) < HEAD_DIM
    zero = jnp.zeros((STRETCH, KV), jnp.bfloat16)

    def stacked(pair):
        return jnp.concatenate([jnp.where(left, pair, zero), jnp.where(left, zero, pair)], axis=0)

    def beside(blocks):
        return jnp.where(left, blocks[:STRETCH], blocks[STRETCH:]).astype(jnp.bfloat16)

    for m in range(NM):
        for copy in dec_copies[m]:
            copy.wait()
        both = dot(encoded, dec_w[m], ((1,), (0,))).astype(jnp.bfloat16)
        keys, values = both[:, :KV], both[:, KV:]
        q = stacked(qg_ref[m, :STRETCH, :])
        g = stacked(qg_ref[m, STRETCH:, :])
        weights = softmax(dot(q, keys, ((1,), (1,))) * SCALE)
        low_w = weights.astype(jnp.bfloat16)
        out_ref[m, :STRETCH, :] = beside(dot(low_w, values, ((1,), (0,))))
        grad_s = softmax_back(weights, dot(g, values, ((1,), (1,)))).astype(jnp.bfloat16)
        out_ref[m, STRETCH:, :] = beside(dot(grad_s, keys, ((1,), (0,))) * SCALE)
        grad_v = dot(low_w, g, ((0,), (0,))).astype(jnp.bfloat16)
        grad_k = (dot(grad_s, q, ((0,), (0,))) * SCALE).astype(jnp.bfloat16)
        term = dot(jnp.concatenate([grad_k, grad_v], axis=1), dec_w[m], ((1,), (1,)))
        if m == 0:
            total_ref[...] = term
        else:
            total_ref[...] += term

    grad_encoded = total_ref[...].astype(jnp.bfloat16)
    for h in range(ENC_HEADS):
        cols = slice(h * HEAD_DIM, (h + 1) * HEAD_DIM)
        keys = kv_ref[:, cols]
        values = kv_ref[:, WIDTH + h * HEAD_DIM : WIDTH + (h + 1) * HEAD_DIM]
        grad_w = dot(grad_encoded[:, cols], values, ((1,), (1,)))
        grad_s = softmax_back(probs_ref[h], grad_w).astype(jnp.bfloat16)
        heads_ref[:, cols] = (dot(grad_s, keys, ((1,), (0,))) * SCALE).astype(jnp.bfloat16)
    back = dot(heads_ref[...], enc_w[...], ((1,), (1,)))
    grad_ref[...] = (grad_encoded.astype(jnp.float32) + back).astype(jnp.bfloat16)


VMEM = pl.BlockSpec(memory_space=pltpu.VMEM)
SMEM = pl.BlockSpec(memory_space=pltpu.SMEM)


def stretch_call(rows, kv, qg, packed):
    return pl.pallas_call(
        stretch_kernel,
        out_shape=(
            jax.ShapeDtypeStruct((NM, 2 * STRETCH, KV), jnp.bfloat16),
            jax.ShapeDtypeStruct((2 * STRETCH, WIDTH), jnp.bfloat16),
        ),
        in_specs=[VMEM, VMEM, VMEM, pl.BlockSpec(memory_space=pl.ANY)],
        out_specs=(VMEM, VMEM),
        scratch_shapes=[
            pltpu.VMEM((WIDTH, WIDTH), jnp.bfloat16),
            pltpu.VMEM((NM, WIDTH, 2 * KV), jnp.bfloat16),
            pltpu.VMEM((2 * STRETCH, WIDTH), jnp.bfloat16),
            pltpu.VMEM((2 * STRETCH, WIDTH), jnp.bfloat16),
            pltpu.VMEM((ENC_HEADS, 2 * STRETCH, STRETCH), jnp.float32),
            pltpu.VMEM((2 * STRETCH, WIDTH), jnp.float32),
            pltpu.SemaphoreType.DMA((NM, 4)),
            pltpu.SemaphoreType.DMA((NM, NC, 2)),
        ],
        compiler_params=pltpu.CompilerParams(vmem_limit_bytes=28 * 1024 * 1024),
        cost_estimate=pl.CostEstimate(
            flops=7_000_000_000, bytes_accessed=11_000_000, transcendentals=200_000
        ),
        name="stretch",
    )(rows, kv, qg, packed)


def choose_kernel(ask_ref, *refs):
    *parts, out_ref, all_ref = refs
    at = 0
    for part in parts:
        all_ref[at : at + part.shape[0]] = part[...]
        at += part.shape[0]

    def copy(i, carry):
        out_ref[i] = all_ref[ask_ref[i]]
        return carry

    lax.fori_loop(0, out_ref.shape[0], copy, 0, unroll=8)


def choose_call(ask, parts):
    return pl.pallas_call(
        choose_kernel,
        out_shape=jax.ShapeDtypeStruct((NX * REQ, SPAN, WIDTH), jnp.bfloat16),
        in_specs=[SMEM] + [VMEM] * len(parts),
        out_specs=VMEM,
        scratch_shapes=[pltpu.VMEM((NC * NZ * SLOTS, SPAN, WIDTH), jnp.bfloat16)],
        compiler_params=pltpu.CompilerParams(vmem_limit_bytes=12 * 1024 * 1024),
        cost_estimate=pl.CostEstimate(flops=0, bytes_accessed=3_000_000, transcendentals=0),
        name="choose",
    )(ask, *parts)


def place_kernel(place_ref, mine_ref, other_ref, *refs):
    *out_refs, total_ref = refs
    total_ref[...] = jnp.zeros_like(total_ref)
    for source, ref in enumerate((mine_ref, other_ref)):

        def add(i, carry, ref=ref, source=source):
            at = place_ref[source, i]
            total_ref[at] += ref[i].astype(jnp.float32)
            return carry

        lax.fori_loop(0, NX * REQ, add, 0, unroll=4)
    at = 0
    for ref in out_refs:
        ref[...] = total_ref[at : at + ref.shape[0]].astype(jnp.bfloat16)
        at += ref.shape[0]


def place_call(place, mine, other):
    return pl.pallas_call(
        place_kernel,
        out_shape=tuple(
            jax.ShapeDtypeStruct((count * SLOTS, SPAN, WIDTH), jnp.bfloat16)
            for count in (1, 2, 2, 2, 1)
        ),
        in_specs=[SMEM, VMEM, VMEM],
        out_specs=(VMEM,) * 5,
        scratch_shapes=[pltpu.VMEM((NONE + 1, SPAN, WIDTH), jnp.float32)],
        compiler_params=pltpu.CompilerParams(vmem_limit_bytes=12 * 1024 * 1024),
        cost_estimate=pl.CostEstimate(
            flops=1_000_000, bytes_accessed=3_000_000, transcendentals=0
        ),
        name="place",
    )(place, mine, other)


def along_z(values, k):
    index = [(z, core) for z in range(NZ) for core in range(NC)]
    pairs = [
        (z * NC + core, (z + (k if core == 0 else -k)) % NZ * NC + core) for z, core in index
    ]
    return lax.ppermute(values, ("z", "core"), pairs)


def shards(queries, stretch_kv, pool, owner, slot, enc_weight, dec_weight, cotangent):
    x, z, core = lax.axis_index("x"), lax.axis_index("z"), lax.axis_index("core")
    swap = [(0, 1), (1, 0)]

    own = lax.dynamic_slice_in_dim(dec_weight, core * HEAD_DIM, HEAD_DIM, axis=2)
    own = own.reshape(WIDTH, KV)
    enc_own = lax.dynamic_slice_in_dim(enc_weight, core * 384, 2 * KV, axis=1)
    packed = jnp.concatenate([own, enc_own[:, :KV], enc_own[:, KV:]], axis=0)
    packed = lax.all_gather(packed, ("core", "mp"), axis=0, tiled=False)

    qg = jnp.concatenate(
        [queries.reshape(NM, STRETCH, KV), cotangent.reshape(NM, STRETCH, KV)], axis=1
    )
    qg = lax.all_to_all(qg, "mp", split_axis=0, concat_axis=0, tiled=True)

    owner = owner.reshape(NX, NZ, NC, REQ)
    slot = slot.reshape(NX, NZ, NC, REQ)
    owner_core = owner % NC
    owner_z = (owner // NC) % NZ
    owner_x = owner // (NC * NZ)
    ahead = (owner_z - z) % NZ
    far = jnp.minimum(ahead, NZ - ahead)
    own_core = owner_core == core
    ask = (
        jnp.where(far == 0, 0, jnp.where(far == 4, 112, far * 32 - 16))
        + jnp.where((far > 0) & (ahead < 4), NC * SLOTS, 0)
        + owner_core * SLOTS
        + slot
    )
    back = jnp.where(core == 0, ahead < 4, ahead > 4) & (far > 0)
    place = slot + jnp.where(
        back,
        far * 2 * SLOTS - SLOTS + jnp.where(own_core, 0, SLOTS),
        jnp.where(own_core & (far == 0), 0, jnp.where(own_core & (far == 4), 56, NONE)),
    )
    place = jnp.where(owner_x == x, jnp.minimum(place, NONE), NONE)

    def of_column(values, which):
        return lax.dynamic_slice(values, (0, z, which, 0), (NX, 1, 1, REQ)).reshape(NX * REQ)

    chip = lax.all_gather(pool, "core", axis=0, tiled=True)
    came = [along_z(chip, k) for k in range(1, 4)] + [along_z(pool, 4)]
    parts = [chip] + [lax.all_gather(part, "core", axis=0, tiled=True) for part in came]
    chosen = choose_call(of_column(ask, core), parts)
    chosen, qg = lax.optimization_barrier((chosen, qg))
    arrived = lax.all_to_all(chosen, "x", split_axis=0, concat_axis=0, tiled=True)
    my_x = lax.dynamic_slice(owner_x, (x, z, core, 0), (1, 1, 1, REQ)).reshape(REQ)
    rows = jnp.take(arrived, my_x * REQ + jnp.arange(REQ), axis=0, mode="clip")
    rows = lax.all_to_all(rows, "mp", split_axis=0, concat_axis=0, tiled=True)
    rows = rows.reshape(2 * STRETCH, WIDTH)
    _, packed = lax.optimization_barrier((chosen, packed))

    out, grad_rows = stretch_call(rows, stretch_kv, qg, packed)

    grad_rows = grad_rows.reshape(REQ, SPAN, WIDTH)
    grad_rows = lax.all_to_all(grad_rows, "mp", split_axis=0, concat_axis=0, tiled=True)
    every = lax.all_gather(grad_rows, "x", axis=0, tiled=True)
    every_beside = lax.ppermute(every, "core", swap)
    places = jnp.stack([of_column(place, core), of_column(place, 1 - core)])
    mine, *partial = place_call(places, every, every_beside)
    partial = [along_z(part, k).astype(jnp.float32) for k, part in enumerate(partial, 1)]
    ours = mine.astype(jnp.float32) + partial[3] + sum(part[:SLOTS] for part in partial[:3])
    theirs = sum(part[SLOTS:] for part in partial[:3]).astype(jnp.bfloat16)
    grad_pool = ours + lax.ppermute(theirs, "core", swap).astype(jnp.float32)

    out = lax.all_to_all(out, "mp", split_axis=0, concat_axis=0, tiled=True)
    attended = out[:, :STRETCH].reshape(NM * STRETCH, KV)
    grad_queries = out[:, STRETCH:].reshape(NM * STRETCH, KV)
    return attended, grad_queries, grad_pool


def solution(mesh):
    split = Mesh(mesh.devices.reshape(NX, NZ, NC, NM), ("x", "z", "core", "mp"))
    in_specs = (
        P(SEQ, "mp"),
        P(SEQ + ("mp",), None),
        P(SEQ, "mp", None),
        P(),
        P(),
        P("mp", None),
        P(None, None, "mp"),
        P(SEQ, "mp"),
    )
    out_specs = (P(SEQ, "mp"), P(SEQ, "mp"), P(SEQ, "mp", None))
    return jax.shard_map(shards, mesh=split, in_specs=in_specs, out_specs=out_specs, check_vma=False)
```

```python
import functools

import jax
import jax.numpy as jnp
from jax import lax
from jax.experimental import pallas as pl
from jax.experimental.pallas import tpu as pltpu
from jax.sharding import Mesh
from jax.sharding import PartitionSpec as P

HEAD_DIM = 128
SCALE = HEAD_DIM ** (-0.5)
SEQ = ("x", "z", "core")
NX, NZ, NC, NM = 4, 8, 2, 8
REQ = 16
SLOTS = 8
STRETCH = 64
SPAN = 8
WIDTH = 896
ENC_HEADS = 7
KV = 2 * HEAD_DIM
ENC_ROWS = 112
NONE = NZ * SLOTS


def dot(a, b, dims):
    return lax.dot_general(a, b, ((dims[0], dims[1]), ((), ())), preferred_element_type=jnp.float32)


def softmax(scores):
    top = jnp.max(scores, axis=-1, keepdims=True)
    e = jnp.exp(scores - top)
    return e * (1.0 / jnp.sum(e, axis=-1, keepdims=True))


def softmax_back(weights, grad):
    return weights * (grad - jnp.sum(grad * weights, axis=-1, keepdims=True))


def stretch_kernel(
    rows_ref,
    kv_ref,
    qg_ref,
    packed_ref,
    out_ref,
    grad_ref,
    enc_parts,
    enc_w,
    dec_w,
    encoded_ref,
    heads_ref,
    probs_ref,
    total_ref,
    enc_sem,
    dec_sem,
):
    enc_copy = pltpu.make_async_copy(
        packed_ref.at[:, pl.ds(WIDTH, 2 * ENC_ROWS), :], enc_parts, enc_sem
    )
    enc_copy.start()
    dec_copies = []
    for m in range(NM):
        group = []
        for core in range(NC):
            group.append(
                pltpu.make_async_copy(
                    packed_ref.at[core * NM + m, pl.ds(0, WIDTH), :],
                    dec_w.at[m, core],
                    dec_sem.at[m, core],
                )
            )
        dec_copies.append(group)
    enc_copy.wait()
    for group in dec_copies:
        for copy in group:
            copy.start()
    for m in range(NM):
        at = slice(m * ENC_ROWS, (m + 1) * ENC_ROWS)
        enc_w[at, :256] = enc_parts[m, :ENC_ROWS]
        enc_w[at, 256:512] = enc_parts[m, ENC_ROWS:]
        enc_w[at, 512:640] = enc_parts[NM + m, :ENC_ROWS, HEAD_DIM:]
        enc_w[at, 640:] = enc_parts[NM + m, ENC_ROWS:]

    rows = rows_ref[...]
    query = dot(rows, enc_w[...], ((1,), (0,))).astype(jnp.bfloat16)
    for h in range(ENC_HEADS):
        cols = slice(h * HEAD_DIM, (h + 1) * HEAD_DIM)
        keys = kv_ref[:, cols]
        values = kv_ref[:, WIDTH + h * HEAD_DIM : WIDTH + (h + 1) * HEAD_DIM]
        weights = softmax(dot(query[:, cols], keys, ((1,), (1,))) * SCALE)
        probs_ref[h] = weights
        mixed = dot(weights.astype(jnp.bfloat16), values, ((1,), (0,)))
        encoded_ref[:, cols] = (rows[:, cols].astype(jnp.float32) + mixed).astype(jnp.bfloat16)
    encoded = encoded_ref[...]

    left = lax.broadcasted_iota(jnp.int32, (STRETCH, KV), 1) < HEAD_DIM
    zero = jnp.zeros((STRETCH, KV), jnp.bfloat16)

    def stacked(pair):
        return jnp.concatenate([jnp.where(left, pair, zero), jnp.where(left, zero, pair)], axis=0)

    def beside(blocks):
        return jnp.where(left, blocks[:STRETCH], blocks[STRETCH:]).astype(jnp.bfloat16)

    for m in range(NM):
        for copy in dec_copies[m]:
            copy.wait()
        pair = [dot(encoded, dec_w[m, h], ((1,), (0,))).astype(jnp.bfloat16) for h in range(2)]
        keys = jnp.concatenate([both[:, :HEAD_DIM] for both in pair], axis=1)
        values = jnp.concatenate([both[:, HEAD_DIM:] for both in pair], axis=1)
        q = stacked(qg_ref[m, :STRETCH, :])
        g = stacked(qg_ref[m, STRETCH:, :])
        weights = softmax(dot(q, keys, ((1,), (1,))) * SCALE)
        low_w = weights.astype(jnp.bfloat16)
        out_ref[m, :STRETCH, :] = beside(dot(low_w, values, ((1,), (0,))))
        grad_s = softmax_back(weights, dot(g, values, ((1,), (1,)))).astype(jnp.bfloat16)
        out_ref[m, STRETCH:, :] = beside(dot(grad_s, keys, ((1,), (0,))) * SCALE)
        grad_v = dot(low_w, g, ((0,), (0,))).astype(jnp.bfloat16)
        grad_k = (dot(grad_s, q, ((0,), (0,))) * SCALE).astype(jnp.bfloat16)
        for h in range(2):
            cols = slice(h * HEAD_DIM, (h + 1) * HEAD_DIM)
            grads = jnp.concatenate([grad_k[:, cols], grad_v[:, cols]], axis=1)
            term = dot(grads, dec_w[m, h], ((1,), (1,)))
            if m == 0 and h == 0:
                total_ref[...] = term
            else:
                total_ref[...] += term

    grad_encoded = total_ref[...].astype(jnp.bfloat16)
    for h in range(ENC_HEADS):
        cols = slice(h * HEAD_DIM, (h + 1) * HEAD_DIM)
        keys = kv_ref[:, cols]
        values = kv_ref[:, WIDTH + h * HEAD_DIM : WIDTH + (h + 1) * HEAD_DIM]
        grad_w = dot(grad_encoded[:, cols], values, ((1,), (1,)))
        grad_s = softmax_back(probs_ref[h], grad_w).astype(jnp.bfloat16)
        heads_ref[:, cols] = (dot(grad_s, keys, ((1,), (0,))) * SCALE).astype(jnp.bfloat16)
    back = dot(heads_ref[...], enc_w[...], ((1,), (1,)))
    grad_ref[...] = (grad_encoded.astype(jnp.float32) + back).astype(jnp.bfloat16)


VMEM = pl.BlockSpec(memory_space=pltpu.VMEM)
SMEM = pl.BlockSpec(memory_space=pltpu.SMEM)


def stretch_call(rows, kv, qg, packed):
    return pl.pallas_call(
        stretch_kernel,
        out_shape=(
            jax.ShapeDtypeStruct((NM, 2 * STRETCH, KV), jnp.bfloat16),
            jax.ShapeDtypeStruct((2 * STRETCH, WIDTH), jnp.bfloat16),
        ),
        in_specs=[VMEM, VMEM, VMEM, pl.BlockSpec(memory_space=pltpu.HBM)],
        out_specs=(VMEM, VMEM),
        scratch_shapes=[
            pltpu.VMEM((NC * NM, 2 * ENC_ROWS, KV), jnp.bfloat16),
            pltpu.VMEM((WIDTH, WIDTH), jnp.bfloat16),
            pltpu.VMEM((NM, NC, WIDTH, KV), jnp.bfloat16),
            pltpu.VMEM((2 * STRETCH, WIDTH), jnp.bfloat16),
            pltpu.VMEM((2 * STRETCH, WIDTH), jnp.bfloat16),
            pltpu.VMEM((ENC_HEADS, 2 * STRETCH, STRETCH), jnp.float32),
            pltpu.VMEM((2 * STRETCH, WIDTH), jnp.float32),
            pltpu.SemaphoreType.DMA,
            pltpu.SemaphoreType.DMA((NM, NC)),
        ],
        compiler_params=pltpu.CompilerParams(vmem_limit_bytes=52 * 1024 * 1024),
        cost_estimate=pl.CostEstimate(
            flops=7_000_000_000, bytes_accessed=11_000_000, transcendentals=200_000
        ),
        name="stretch",
    )(rows, kv, qg, packed)


def choose_kernel(count, ask_ref, *refs):
    parts, out_refs, all_ref = refs[:count], refs[count:-1], refs[-1]
    at = 0
    for part in parts:
        all_ref[at : at + part.shape[0]] = part[...]
        at += part.shape[0]
    for number, out_ref in enumerate(out_refs):

        def copy(i, carry, number=number, out_ref=out_ref):
            out_ref[i] = all_ref[ask_ref[number * REQ + i]]
            return carry

        lax.fori_loop(0, REQ, copy, 0, unroll=8)


def choose_call(ask, parts):
    outs = ask.shape[0] // REQ
    total = sum(part.shape[0] for part in parts)
    return pl.pallas_call(
        functools.partial(choose_kernel, len(parts)),
        out_shape=(jax.ShapeDtypeStruct((REQ, SPAN, WIDTH), jnp.bfloat16),) * outs,
        in_specs=[SMEM] + [VMEM] * len(parts),
        out_specs=(VMEM,) * outs,
        scratch_shapes=[pltpu.VMEM((total, SPAN, WIDTH), jnp.bfloat16)],
        compiler_params=pltpu.CompilerParams(vmem_limit_bytes=12 * 1024 * 1024),
        cost_estimate=pl.CostEstimate(flops=0, bytes_accessed=3_000_000, transcendentals=0),
        name="choose",
    )(ask, *parts)


def place_kernel(place_ref, mine_ref, other_ref, *refs):
    *out_refs, total_ref = refs
    total_ref[...] = jnp.zeros_like(total_ref)
    for source, ref in enumerate((mine_ref, other_ref)):

        def add(i, carry, ref=ref, source=source):
            at = place_ref[source, i]
            total_ref[at] += ref[i].astype(jnp.float32)
            return carry

        lax.fori_loop(0, NX * REQ, add, 0, unroll=4)
    at = 0
    for ref in out_refs:
        ref[...] = total_ref[at : at + ref.shape[0]].astype(jnp.bfloat16)
        at += ref.shape[0]


def place_call(place, mine, other):
    return pl.pallas_call(
        place_kernel,
        out_shape=tuple(
            jax.ShapeDtypeStruct((count * SLOTS, SPAN, WIDTH), jnp.bfloat16)
            for count in (1, 2, 2, 2, 1)
        ),
        in_specs=[SMEM, VMEM, VMEM],
        out_specs=(VMEM,) * 5,
        scratch_shapes=[pltpu.VMEM((NONE + 1, SPAN, WIDTH), jnp.float32)],
        compiler_params=pltpu.CompilerParams(vmem_limit_bytes=12 * 1024 * 1024),
        cost_estimate=pl.CostEstimate(
            flops=1_000_000, bytes_accessed=3_000_000, transcendentals=0
        ),
        name="place",
    )(place, mine, other)


def along_z(values, k):
    index = [(z, core) for z in range(NZ) for core in range(NC)]
    pairs = [
        (z * NC + core, (z + (k if core == 0 else -k)) % NZ * NC + core) for z, core in index
    ]
    return lax.ppermute(values, ("z", "core"), pairs)


def shards(queries, stretch_kv, pool, owner, slot, enc_weight, dec_weight, cotangent):
    x, z, core = lax.axis_index("x"), lax.axis_index("z"), lax.axis_index("core")
    swap = [(0, 1), (1, 0)]

    own = lax.dynamic_slice_in_dim(dec_weight, core * HEAD_DIM, HEAD_DIM, axis=2)
    own = own.reshape(WIDTH, KV)
    enc_own = lax.dynamic_slice_in_dim(enc_weight, core * 384, 2 * KV, axis=1)
    packed = jnp.concatenate([own, enc_own[:, :KV], enc_own[:, KV:]], axis=0)
    packed = lax.all_gather(packed, ("core", "mp"), axis=0, tiled=False)

    qg = jnp.concatenate(
        [queries.reshape(NM, STRETCH, KV), cotangent.reshape(NM, STRETCH, KV)], axis=1
    )
    qg = lax.all_to_all(qg, "mp", split_axis=0, concat_axis=0, tiled=True)

    owner = owner.reshape(NX, NZ, NC, REQ)
    slot = slot.reshape(NX, NZ, NC, REQ)
    owner_core = owner % NC
    owner_z = (owner // NC) % NZ
    owner_x = owner // (NC * NZ)
    ahead = (owner_z - z) % NZ
    far = jnp.minimum(ahead, NZ - ahead)
    own_core = owner_core == core
    ask = (
        jnp.where(far == 0, 0, jnp.where(far == 4, 112, far * 32 - 16))
        + jnp.where((far > 0) & (ahead < 4), NC * SLOTS, 0)
        + owner_core * SLOTS
        + slot
    )
    back = jnp.where(core == 0, ahead < 4, ahead > 4) & (far > 0)
    place = slot + jnp.where(
        back,
        far * 2 * SLOTS - SLOTS + jnp.where(own_core, 0, SLOTS),
        jnp.where(own_core & (far == 0), 0, jnp.where(own_core & (far == 4), 56, NONE)),
    )
    place = jnp.where(owner_x == x, jnp.minimum(place, NONE), NONE)

    def of_column(values, which):
        return lax.dynamic_slice(values, (0, z, which, 0), (NX, 1, 1, REQ)).reshape(NX * REQ)

    chip = lax.all_gather(pool, "core", axis=0, tiled=True)
    came = [along_z(chip, k) for k in range(1, 4)] + [along_z(pool, 4)]
    parts = [chip] + [lax.all_gather(part, "core", axis=0, tiled=True) for part in came]
    ask = of_column(ask, core).reshape(NX, REQ)
    ask = jnp.take(ask, (x + jnp.arange(NX)) % NX, axis=0, mode="clip").reshape(NX * REQ)
    chosen = choose_call(ask, parts)
    arrived = [chosen[0]] + [
        lax.ppermute(chosen[k], "x", [(i, (i + k) % NX) for i in range(NX)]) for k in range(1, NX)
    ]
    my_x = lax.dynamic_slice(owner_x, (x, z, core, 0), (1, 1, 1, REQ)).reshape(REQ)
    (rows,) = choose_call((x - my_x) % NX * REQ + jnp.arange(REQ), arrived)
    rows, qg = lax.optimization_barrier((rows, qg))
    rows = lax.all_to_all(rows, "mp", split_axis=0, concat_axis=0, tiled=True)
    rows = rows.reshape(2 * STRETCH, WIDTH)
    _, packed = lax.optimization_barrier((chosen[0], packed))

    out, grad_rows = stretch_call(rows, stretch_kv, qg, packed)

    grad_rows = grad_rows.reshape(REQ, SPAN, WIDTH)
    grad_rows = lax.all_to_all(grad_rows, "mp", split_axis=0, concat_axis=0, tiled=True)
    every = lax.all_gather(grad_rows, "x", axis=0, tiled=True)
    every_beside = lax.ppermute(every, "core", swap)
    places = jnp.stack([of_column(place, core), of_column(place, 1 - core)])
    mine, *partial = place_call(places, every, every_beside)
    partial = [along_z(part, k) for k, part in enumerate(partial, 1)]
    partial = [part.astype(jnp.float32) for part in lax.optimization_barrier(partial)]
    ours = mine.astype(jnp.float32) + partial[3] + sum(part[:SLOTS] for part in partial[:3])
    theirs = sum(part[SLOTS:] for part in partial[:3]).astype(jnp.bfloat16)
    theirs = lax.all_gather(theirs, "core", axis=0, tiled=False)
    theirs = lax.dynamic_index_in_dim(theirs, 1 - core, 0, keepdims=False)
    grad_pool = ours + theirs.astype(jnp.float32)

    out = lax.all_to_all(out, "mp", split_axis=0, concat_axis=0, tiled=True)
    attended = out[:, :STRETCH].reshape(NM * STRETCH, KV)
    grad_queries = out[:, STRETCH:].reshape(NM * STRETCH, KV)
    return attended, grad_queries, grad_pool


def solution(mesh):
    split = Mesh(mesh.devices.reshape(NX, NZ, NC, NM), ("x", "z", "core", "mp"))
    in_specs = (
        P(SEQ, "mp"),
        P(SEQ + ("mp",), None),
        P(SEQ, "mp", None),
        P(),
        P(),
        P("mp", None),
        P(None, None, "mp"),
        P(SEQ, "mp"),
    )
    out_specs = (P(SEQ, "mp"), P(SEQ, "mp"), P(SEQ, "mp", None))
    return jax.shard_map(shards, mesh=split, in_specs=in_specs, out_specs=out_specs, check_vma=False)
```

```python
import functools

import jax
import jax.numpy as jnp
from jax import lax
from jax.experimental import pallas as pl
from jax.experimental.pallas import tpu as pltpu
from jax.sharding import Mesh
from jax.sharding import PartitionSpec as P

HEAD_DIM = 128
SCALE = HEAD_DIM ** (-0.5)
SEQ = ("x", "z", "core")
NX, NZ, NC, NM = 4, 8, 2, 8
REQ = 16
SLOTS = 8
STRETCH = 64
SPAN = 8
WIDTH = 896
ENC_HEADS = 7
KV = 2 * HEAD_DIM
ENC_ROWS = 112
NONE = NZ * SLOTS


def dot(a, b, dims):
    return lax.dot_general(a, b, ((dims[0], dims[1]), ((), ())), preferred_element_type=jnp.float32)


def softmax(scores):
    top = jnp.max(scores, axis=-1, keepdims=True)
    e = jnp.exp(scores - top)
    return e * (1.0 / jnp.sum(e, axis=-1, keepdims=True))


def softmax_back(weights, grad):
    return weights * (grad - jnp.sum(grad * weights, axis=-1, keepdims=True))


def stretch_kernel(
    rows_ref,
    kv_ref,
    qg_ref,
    packed_ref,
    out_ref,
    grad_ref,
    enc_parts,
    enc_w,
    dec_w,
    encoded_ref,
    heads_ref,
    probs_ref,
    total_ref,
    enc_sem,
    dec_sem,
):
    enc_copy = pltpu.make_async_copy(
        packed_ref.at[:, pl.ds(WIDTH, 2 * ENC_ROWS), :], enc_parts, enc_sem
    )
    enc_copy.start()
    dec_copies = []
    for m in range(NM):
        group = []
        for core in range(NC):
            group.append(
                pltpu.make_async_copy(
                    packed_ref.at[core * NM + m, pl.ds(0, WIDTH), :],
                    dec_w.at[m, core],
                    dec_sem.at[m, core],
                )
            )
        dec_copies.append(group)
    enc_copy.wait()
    for group in dec_copies:
        for copy in group:
            copy.start()
    for m in range(NM):
        at = slice(m * ENC_ROWS, (m + 1) * ENC_ROWS)
        enc_w[at, :256] = enc_parts[m, :ENC_ROWS]
        enc_w[at, 256:512] = enc_parts[m, ENC_ROWS:]
        enc_w[at, 512:640] = enc_parts[NM + m, :ENC_ROWS, HEAD_DIM:]
        enc_w[at, 640:] = enc_parts[NM + m, ENC_ROWS:]

    rows = rows_ref[...]
    query = dot(rows, enc_w[...], ((1,), (0,))).astype(jnp.bfloat16)
    for h in range(ENC_HEADS):
        cols = slice(h * HEAD_DIM, (h + 1) * HEAD_DIM)
        keys = kv_ref[:, cols]
        values = kv_ref[:, WIDTH + h * HEAD_DIM : WIDTH + (h + 1) * HEAD_DIM]
        weights = softmax(dot(query[:, cols], keys, ((1,), (1,))) * SCALE)
        probs_ref[h] = weights
        mixed = dot(weights.astype(jnp.bfloat16), values, ((1,), (0,)))
        encoded_ref[:, cols] = (rows[:, cols].astype(jnp.float32) + mixed).astype(jnp.bfloat16)
    encoded = encoded_ref[...]

    left = lax.broadcasted_iota(jnp.int32, (STRETCH, KV), 1) < HEAD_DIM
    zero = jnp.zeros((STRETCH, KV), jnp.bfloat16)

    def stacked(pair):
        return jnp.concatenate([jnp.where(left, pair, zero), jnp.where(left, zero, pair)], axis=0)

    def beside(blocks):
        return jnp.where(left, blocks[:STRETCH], blocks[STRETCH:]).astype(jnp.bfloat16)

    for m in range(NM):
        for copy in dec_copies[m]:
            copy.wait()
        pair = [dot(encoded, dec_w[m, h], ((1,), (0,))).astype(jnp.bfloat16) for h in range(2)]
        keys = jnp.concatenate([both[:, :HEAD_DIM] for both in pair], axis=1)
        values = jnp.concatenate([both[:, HEAD_DIM:] for both in pair], axis=1)
        q = stacked(qg_ref[m, :STRETCH, :])
        g = stacked(qg_ref[m, STRETCH:, :])
        weights = softmax(dot(q, keys, ((1,), (1,))) * SCALE)
        low_w = weights.astype(jnp.bfloat16)
        out_ref[m, :STRETCH, :] = beside(dot(low_w, values, ((1,), (0,))))
        grad_s = softmax_back(weights, dot(g, values, ((1,), (1,)))).astype(jnp.bfloat16)
        out_ref[m, STRETCH:, :] = beside(dot(grad_s, keys, ((1,), (0,))) * SCALE)
        grad_v = dot(low_w, g, ((0,), (0,))).astype(jnp.bfloat16)
        grad_k = (dot(grad_s, q, ((0,), (0,))) * SCALE).astype(jnp.bfloat16)
        for h in range(2):
            cols = slice(h * HEAD_DIM, (h + 1) * HEAD_DIM)
            grads = jnp.concatenate([grad_k[:, cols], grad_v[:, cols]], axis=1)
            term = dot(grads, dec_w[m, h], ((1,), (1,)))
            if m == 0 and h == 0:
                total_ref[...] = term
            else:
                total_ref[...] += term

    grad_encoded = total_ref[...].astype(jnp.bfloat16)
    for h in range(ENC_HEADS):
        cols = slice(h * HEAD_DIM, (h + 1) * HEAD_DIM)
        keys = kv_ref[:, cols]
        values = kv_ref[:, WIDTH + h * HEAD_DIM : WIDTH + (h + 1) * HEAD_DIM]
        grad_w = dot(grad_encoded[:, cols], values, ((1,), (1,)))
        grad_s = softmax_back(probs_ref[h], grad_w).astype(jnp.bfloat16)
        heads_ref[:, cols] = (dot(grad_s, keys, ((1,), (0,))) * SCALE).astype(jnp.bfloat16)
    back = dot(heads_ref[...], enc_w[...], ((1,), (1,)))
    grad_ref[...] = (grad_encoded.astype(jnp.float32) + back).astype(jnp.bfloat16)


VMEM = pl.BlockSpec(memory_space=pltpu.VMEM)
SMEM = pl.BlockSpec(memory_space=pltpu.SMEM)


def stretch_call(rows, kv, qg, packed):
    return pl.pallas_call(
        stretch_kernel,
        out_shape=(
            jax.ShapeDtypeStruct((NM, 2 * STRETCH, KV), jnp.bfloat16),
            jax.ShapeDtypeStruct((2 * STRETCH, WIDTH), jnp.bfloat16),
        ),
        in_specs=[VMEM, VMEM, VMEM, pl.BlockSpec(memory_space=pltpu.HBM)],
        out_specs=(VMEM, VMEM),
        scratch_shapes=[
            pltpu.VMEM((NC * NM, 2 * ENC_ROWS, KV), jnp.bfloat16),
            pltpu.VMEM((WIDTH, WIDTH), jnp.bfloat16),
            pltpu.VMEM((NM, NC, WIDTH, KV), jnp.bfloat16),
            pltpu.VMEM((2 * STRETCH, WIDTH), jnp.bfloat16),
            pltpu.VMEM((2 * STRETCH, WIDTH), jnp.bfloat16),
            pltpu.VMEM((ENC_HEADS, 2 * STRETCH, STRETCH), jnp.float32),
            pltpu.VMEM((2 * STRETCH, WIDTH), jnp.float32),
            pltpu.SemaphoreType.DMA,
            pltpu.SemaphoreType.DMA((NM, NC)),
        ],
        compiler_params=pltpu.CompilerParams(vmem_limit_bytes=52 * 1024 * 1024),
        cost_estimate=pl.CostEstimate(
            flops=7_000_000_000, bytes_accessed=11_000_000, transcendentals=200_000
        ),
        name="stretch",
    )(rows, kv, qg, packed)


def choose_kernel(count, ask_ref, *refs):
    parts, out_refs, all_ref = refs[:count], refs[count:-1], refs[-1]
    at = 0
    for part in parts:
        all_ref[at : at + part.shape[0]] = part[...]
        at += part.shape[0]
    for number, out_ref in enumerate(out_refs):

        def copy(i, carry, number=number, out_ref=out_ref):
            out_ref[i] = all_ref[ask_ref[number * REQ + i]]
            return carry

        lax.fori_loop(0, REQ, copy, 0, unroll=8)


def choose_call(ask, parts):
    outs = ask.shape[0] // REQ
    total = sum(part.shape[0] for part in parts)
    return pl.pallas_call(
        functools.partial(choose_kernel, len(parts)),
        out_shape=(jax.ShapeDtypeStruct((REQ, SPAN, WIDTH), jnp.bfloat16),) * outs,
        in_specs=[SMEM] + [VMEM] * len(parts),
        out_specs=(VMEM,) * outs,
        scratch_shapes=[pltpu.VMEM((total, SPAN, WIDTH), jnp.bfloat16)],
        compiler_params=pltpu.CompilerParams(vmem_limit_bytes=12 * 1024 * 1024),
        cost_estimate=pl.CostEstimate(flops=0, bytes_accessed=3_000_000, transcendentals=0),
        name="choose",
    )(ask, *parts)


def place_kernel(place_ref, mine_ref, other_ref, *refs):
    *out_refs, total_ref = refs
    total_ref[...] = jnp.zeros_like(total_ref)
    for source, ref in enumerate((mine_ref, other_ref)):

        def add(i, carry, ref=ref, source=source):
            at = place_ref[source, i]
            total_ref[at] += ref[i].astype(jnp.float32)
            return carry

        lax.fori_loop(0, NX * REQ, add, 0, unroll=4)
    at = 0
    for ref in out_refs:
        ref[...] = total_ref[at : at + ref.shape[0]].astype(jnp.bfloat16)
        at += ref.shape[0]


def place_call(place, mine, other):
    return pl.pallas_call(
        place_kernel,
        out_shape=tuple(
            jax.ShapeDtypeStruct((count * SLOTS, SPAN, WIDTH), jnp.bfloat16)
            for count in (1, 2, 2, 2, 1)
        ),
        in_specs=[SMEM, VMEM, VMEM],
        out_specs=(VMEM,) * 5,
        scratch_shapes=[pltpu.VMEM((NONE + 1, SPAN, WIDTH), jnp.float32)],
        compiler_params=pltpu.CompilerParams(vmem_limit_bytes=12 * 1024 * 1024),
        cost_estimate=pl.CostEstimate(
            flops=1_000_000, bytes_accessed=3_000_000, transcendentals=0
        ),
        name="place",
    )(place, mine, other)


def join_kernel(core_ref, mine_ref, other_ref, out_ref):
    core = core_ref[0]
    out_ref[pl.ds(core * SLOTS, SLOTS)] = mine_ref[...]
    out_ref[pl.ds((1 - core) * SLOTS, SLOTS)] = other_ref[...]


def join_call(core, mine, other):
    return pl.pallas_call(
        join_kernel,
        out_shape=jax.ShapeDtypeStruct((NC * SLOTS, SPAN, WIDTH), jnp.bfloat16),
        in_specs=[SMEM, VMEM, VMEM],
        out_specs=VMEM,
        compiler_params=pltpu.CompilerParams(vmem_limit_bytes=4 * 1024 * 1024),
        cost_estimate=pl.CostEstimate(flops=0, bytes_accessed=460_000, transcendentals=0),
        name="join",
    )(core, mine, other)


def along_z(values, k):
    index = [(z, core) for z in range(NZ) for core in range(NC)]
    pairs = [
        (z * NC + core, (z + (k if core == 0 else -k)) % NZ * NC + core) for z, core in index
    ]
    return lax.ppermute(values, ("z", "core"), pairs)


def shards(queries, stretch_kv, pool, owner, slot, enc_weight, dec_weight, cotangent):
    x, z, core = lax.axis_index("x"), lax.axis_index("z"), lax.axis_index("core")
    swap = [(0, 1), (1, 0)]

    own = lax.dynamic_slice_in_dim(dec_weight, core * HEAD_DIM, HEAD_DIM, axis=2)
    own = own.reshape(WIDTH, KV)
    enc_own = lax.dynamic_slice_in_dim(enc_weight, core * 384, 2 * KV, axis=1)
    packed = jnp.concatenate([own, enc_own[:, :KV], enc_own[:, KV:]], axis=0)
    packed = lax.all_gather(packed, ("core", "mp"), axis=0, tiled=False)

    qg = jnp.concatenate(
        [queries.reshape(NM, STRETCH, KV), cotangent.reshape(NM, STRETCH, KV)], axis=1
    )
    qg = lax.all_to_all(qg, "mp", split_axis=0, concat_axis=0, tiled=True)

    owner = owner.reshape(NX, NZ, NC, REQ)
    slot = slot.reshape(NX, NZ, NC, REQ)
    owner_core = owner % NC
    owner_z = (owner // NC) % NZ
    owner_x = owner // (NC * NZ)
    ahead = (owner_z - z) % NZ
    far = jnp.minimum(ahead, NZ - ahead)
    own_core = owner_core == core
    ask = (
        jnp.where(far == 0, 0, jnp.where(far == 4, 112, far * 32 - 16))
        + jnp.where((far > 0) & (ahead < 4), NC * SLOTS, 0)
        + owner_core * SLOTS
        + slot
    )
    back = jnp.where(core == 0, ahead < 4, ahead > 4) & (far > 0)
    place = slot + jnp.where(
        back,
        far * 2 * SLOTS - SLOTS + jnp.where(own_core, 0, SLOTS),
        jnp.where(own_core & (far == 0), 0, jnp.where(own_core & (far == 4), 56, NONE)),
    )
    place = jnp.where(owner_x == x, jnp.minimum(place, NONE), NONE)

    def of_column(values, which):
        return lax.dynamic_slice(values, (0, z, which, 0), (NX, 1, 1, REQ)).reshape(NX * REQ)

    beside = lax.ppermute(pool, "core", swap)
    chip = join_call(core.reshape(1).astype(jnp.int32), pool, beside)
    own_pool, _ = lax.optimization_barrier((pool, chip))
    came = [along_z(chip, k) for k in range(1, 4)] + [along_z(own_pool, 4)]
    parts = [chip] + [lax.all_gather(part, "core", axis=0, tiled=True) for part in came]
    ask = of_column(ask, core).reshape(NX, REQ)
    ask = jnp.take(ask, (x + jnp.arange(NX)) % NX, axis=0, mode="clip").reshape(NX * REQ)
    chosen = choose_call(ask, parts)
    arrived = [chosen[0]] + [
        lax.ppermute(chosen[k], "x", [(i, (i + k) % NX) for i in range(NX)]) for k in range(1, NX)
    ]
    my_x = lax.dynamic_slice(owner_x, (x, z, core, 0), (1, 1, 1, REQ)).reshape(REQ)
    (rows,) = choose_call((x - my_x) % NX * REQ + jnp.arange(REQ), arrived)
    rows, qg = lax.optimization_barrier((rows, qg))
    rows = lax.all_to_all(rows, "mp", split_axis=0, concat_axis=0, tiled=True)
    rows = rows.reshape(2 * STRETCH, WIDTH)
    _, packed = lax.optimization_barrier((chosen[0], packed))

    out, grad_rows = stretch_call(rows, stretch_kv, qg, packed)

    grad_rows = grad_rows.reshape(REQ, SPAN, WIDTH)
    grad_rows = lax.all_to_all(grad_rows, "mp", split_axis=0, concat_axis=0, tiled=True)
    every = lax.all_gather(grad_rows, "x", axis=0, tiled=True)
    every_beside = lax.ppermute(every, "core", swap)
    places = jnp.stack([of_column(place, core), of_column(place, 1 - core)])
    mine, *partial = place_call(places, every, every_beside)
    partial = [along_z(part, k) for k, part in enumerate(partial, 1)]
    partial = [part.astype(jnp.float32) for part in lax.optimization_barrier(partial)]
    ours = mine.astype(jnp.float32) + partial[3] + sum(part[:SLOTS] for part in partial[:3])
    theirs = sum(part[SLOTS:] for part in partial[:3]).astype(jnp.bfloat16)
    theirs = lax.all_gather(theirs, "core", axis=0, tiled=False)
    theirs = lax.dynamic_index_in_dim(theirs, 1 - core, 0, keepdims=False)
    grad_pool = ours + theirs.astype(jnp.float32)

    out = lax.all_to_all(out, "mp", split_axis=0, concat_axis=0, tiled=True)
    attended = out[:, :STRETCH].reshape(NM * STRETCH, KV)
    grad_queries = out[:, STRETCH:].reshape(NM * STRETCH, KV)
    return attended, grad_queries, grad_pool


def solution(mesh):
    split = Mesh(mesh.devices.reshape(NX, NZ, NC, NM), ("x", "z", "core", "mp"))
    in_specs = (
        P(SEQ, "mp"),
        P(SEQ + ("mp",), None),
        P(SEQ, "mp", None),
        P(),
        P(),
        P("mp", None),
        P(None, None, "mp"),
        P(SEQ, "mp"),
    )
    out_specs = (P(SEQ, "mp"), P(SEQ, "mp"), P(SEQ, "mp", None))
    return jax.shard_map(shards, mesh=split, in_specs=in_specs, out_specs=out_specs, check_vma=False)
```

```python
import functools

import jax
import jax.numpy as jnp
from jax import lax
from jax.experimental import pallas as pl
from jax.experimental.pallas import tpu as pltpu
from jax.sharding import Mesh
from jax.sharding import PartitionSpec as P

HEAD_DIM = 128
SCALE = HEAD_DIM ** (-0.5)
SEQ = ("x", "z", "core")
NX, NZ, NC, NM = 4, 8, 2, 8
REQ = 16
SLOTS = 8
STRETCH = 64
SPAN = 8
WIDTH = 896
ENC_HEADS = 7
KV = 2 * HEAD_DIM
ENC_ROWS = 112
NONE = NZ * SLOTS


def dot(a, b, dims):
    return lax.dot_general(a, b, ((dims[0], dims[1]), ((), ())), preferred_element_type=jnp.float32)


def softmax(scores):
    top = jnp.max(scores, axis=-1, keepdims=True)
    e = jnp.exp(scores - top)
    return e * (1.0 / jnp.sum(e, axis=-1, keepdims=True))


def softmax_back(weights, grad):
    return weights * (grad - jnp.sum(grad * weights, axis=-1, keepdims=True))


def stretch_kernel(
    rows_ref,
    kv_ref,
    qg_ref,
    packed_ref,
    out_ref,
    grad_ref,
    enc_parts,
    enc_w,
    dec_w,
    encoded_ref,
    heads_ref,
    probs_ref,
    total_ref,
    enc_sem,
    dec_sem,
):
    enc_copy = pltpu.make_async_copy(
        packed_ref.at[:, pl.ds(WIDTH, 2 * ENC_ROWS), :], enc_parts, enc_sem
    )
    enc_copy.start()
    dec_copies = []
    for m in range(NM):
        group = []
        for core in range(NC):
            group.append(
                pltpu.make_async_copy(
                    packed_ref.at[core * NM + m, pl.ds(0, WIDTH), :],
                    dec_w.at[m, core],
                    dec_sem.at[m, core],
                )
            )
        dec_copies.append(group)
    enc_copy.wait()
    for group in dec_copies:
        for copy in group:
            copy.start()
    for m in range(NM):
        at = slice(m * ENC_ROWS, (m + 1) * ENC_ROWS)
        enc_w[at, :256] = enc_parts[m, :ENC_ROWS]
        enc_w[at, 256:512] = enc_parts[m, ENC_ROWS:]
        enc_w[at, 512:640] = enc_parts[NM + m, :ENC_ROWS, HEAD_DIM:]
        enc_w[at, 640:] = enc_parts[NM + m, ENC_ROWS:]

    rows = rows_ref[...]
    query = dot(rows, enc_w[...], ((1,), (0,))).astype(jnp.bfloat16)
    for h in range(ENC_HEADS):
        cols = slice(h * HEAD_DIM, (h + 1) * HEAD_DIM)
        keys = kv_ref[:, cols]
        values = kv_ref[:, WIDTH + h * HEAD_DIM : WIDTH + (h + 1) * HEAD_DIM]
        weights = softmax(dot(query[:, cols], keys, ((1,), (1,))) * SCALE)
        probs_ref[h] = weights
        mixed = dot(weights.astype(jnp.bfloat16), values, ((1,), (0,)))
        encoded_ref[:, cols] = (rows[:, cols].astype(jnp.float32) + mixed).astype(jnp.bfloat16)
    encoded = encoded_ref[...]

    left = lax.broadcasted_iota(jnp.int32, (STRETCH, KV), 1) < HEAD_DIM
    zero = jnp.zeros((STRETCH, KV), jnp.bfloat16)

    def stacked(pair):
        return jnp.concatenate([jnp.where(left, pair, zero), jnp.where(left, zero, pair)], axis=0)

    def beside(blocks):
        return jnp.where(left, blocks[:STRETCH], blocks[STRETCH:]).astype(jnp.bfloat16)

    for m in range(NM):
        for copy in dec_copies[m]:
            copy.wait()
        pair = [dot(encoded, dec_w[m, h], ((1,), (0,))).astype(jnp.bfloat16) for h in range(2)]
        keys = jnp.concatenate([both[:, :HEAD_DIM] for both in pair], axis=1)
        values = jnp.concatenate([both[:, HEAD_DIM:] for both in pair], axis=1)
        q = stacked(qg_ref[m, :STRETCH, :])
        g = stacked(qg_ref[m, STRETCH:, :])
        weights = softmax(dot(q, keys, ((1,), (1,))) * SCALE)
        low_w = weights.astype(jnp.bfloat16)
        out_ref[m, :STRETCH, :] = beside(dot(low_w, values, ((1,), (0,))))
        grad_s = softmax_back(weights, dot(g, values, ((1,), (1,)))).astype(jnp.bfloat16)
        out_ref[m, STRETCH:, :] = beside(dot(grad_s, keys, ((1,), (0,))) * SCALE)
        grad_v = dot(low_w, g, ((0,), (0,))).astype(jnp.bfloat16)
        grad_k = (dot(grad_s, q, ((0,), (0,))) * SCALE).astype(jnp.bfloat16)
        for h in range(2):
            cols = slice(h * HEAD_DIM, (h + 1) * HEAD_DIM)
            grads = jnp.concatenate([grad_k[:, cols], grad_v[:, cols]], axis=1)
            term = dot(grads, dec_w[m, h], ((1,), (1,)))
            if m == 0 and h == 0:
                total_ref[...] = term
            else:
                total_ref[...] += term

    grad_encoded = total_ref[...].astype(jnp.bfloat16)
    for h in range(ENC_HEADS):
        cols = slice(h * HEAD_DIM, (h + 1) * HEAD_DIM)
        keys = kv_ref[:, cols]
        values = kv_ref[:, WIDTH + h * HEAD_DIM : WIDTH + (h + 1) * HEAD_DIM]
        grad_w = dot(grad_encoded[:, cols], values, ((1,), (1,)))
        grad_s = softmax_back(probs_ref[h], grad_w).astype(jnp.bfloat16)
        heads_ref[:, cols] = (dot(grad_s, keys, ((1,), (0,))) * SCALE).astype(jnp.bfloat16)
    back = dot(heads_ref[...], enc_w[...], ((1,), (1,)))
    grad_ref[...] = (grad_encoded.astype(jnp.float32) + back).astype(jnp.bfloat16)


VMEM = pl.BlockSpec(memory_space=pltpu.VMEM)
SMEM = pl.BlockSpec(memory_space=pltpu.SMEM)


def stretch_call(rows, kv, qg, packed):
    return pl.pallas_call(
        stretch_kernel,
        out_shape=(
            jax.ShapeDtypeStruct((NM, 2 * STRETCH, KV), jnp.bfloat16),
            jax.ShapeDtypeStruct((2 * STRETCH, WIDTH), jnp.bfloat16),
        ),
        in_specs=[VMEM, VMEM, VMEM, pl.BlockSpec(memory_space=pltpu.HBM)],
        out_specs=(VMEM, VMEM),
        scratch_shapes=[
            pltpu.VMEM((NC * NM, 2 * ENC_ROWS, KV), jnp.bfloat16),
            pltpu.VMEM((WIDTH, WIDTH), jnp.bfloat16),
            pltpu.VMEM((NM, NC, WIDTH, KV), jnp.bfloat16),
            pltpu.VMEM((2 * STRETCH, WIDTH), jnp.bfloat16),
            pltpu.VMEM((2 * STRETCH, WIDTH), jnp.bfloat16),
            pltpu.VMEM((ENC_HEADS, 2 * STRETCH, STRETCH), jnp.float32),
            pltpu.VMEM((2 * STRETCH, WIDTH), jnp.float32),
            pltpu.SemaphoreType.DMA,
            pltpu.SemaphoreType.DMA((NM, NC)),
        ],
        compiler_params=pltpu.CompilerParams(vmem_limit_bytes=52 * 1024 * 1024),
        cost_estimate=pl.CostEstimate(
            flops=7_000_000_000, bytes_accessed=11_000_000, transcendentals=200_000
        ),
        name="stretch",
    )(rows, kv, qg, packed)


def choose_kernel(count, ask_ref, *refs):
    parts, out_refs, all_ref = refs[:count], refs[count:-1], refs[-1]
    at = 0
    for part in parts:
        all_ref[at : at + part.shape[0]] = part[...]
        at += part.shape[0]
    for number, out_ref in enumerate(out_refs):

        def copy(i, carry, number=number, out_ref=out_ref):
            out_ref[i] = all_ref[ask_ref[number * REQ + i]]
            return carry

        lax.fori_loop(0, REQ, copy, 0, unroll=8)


def choose_call(ask, parts):
    outs = ask.shape[0] // REQ
    total = sum(part.shape[0] for part in parts)
    return pl.pallas_call(
        functools.partial(choose_kernel, len(parts)),
        out_shape=(jax.ShapeDtypeStruct((REQ, SPAN, WIDTH), jnp.bfloat16),) * outs,
        in_specs=[SMEM] + [VMEM] * len(parts),
        out_specs=(VMEM,) * outs,
        scratch_shapes=[pltpu.VMEM((total, SPAN, WIDTH), jnp.bfloat16)],
        compiler_params=pltpu.CompilerParams(vmem_limit_bytes=12 * 1024 * 1024),
        cost_estimate=pl.CostEstimate(flops=0, bytes_accessed=3_000_000, transcendentals=0),
        name="choose",
    )(ask, *parts)


def place_kernel(place_ref, mine_ref, other_ref, *refs):
    *out_refs, total_ref = refs
    total_ref[...] = jnp.zeros_like(total_ref)
    for source, ref in enumerate((mine_ref, other_ref)):

        def add(i, carry, ref=ref, source=source):
            at = place_ref[source, i]
            total_ref[at] += ref[i].astype(jnp.float32)
            return carry

        lax.fori_loop(0, NX * REQ, add, 0, unroll=4)
    at = 0
    for ref in out_refs:
        ref[...] = total_ref[at : at + ref.shape[0]].astype(jnp.bfloat16)
        at += ref.shape[0]


def place_call(place, mine, other):
    return pl.pallas_call(
        place_kernel,
        out_shape=tuple(
            jax.ShapeDtypeStruct((count * SLOTS, SPAN, WIDTH), jnp.bfloat16)
            for count in (1, 2, 2, 2, 1)
        ),
        in_specs=[SMEM, VMEM, VMEM],
        out_specs=(VMEM,) * 5,
        scratch_shapes=[pltpu.VMEM((NONE + 1, SPAN, WIDTH), jnp.float32)],
        compiler_params=pltpu.CompilerParams(vmem_limit_bytes=12 * 1024 * 1024),
        cost_estimate=pl.CostEstimate(
            flops=1_000_000, bytes_accessed=3_000_000, transcendentals=0
        ),
        name="place",
    )(place, mine, other)


def join_kernel(core_ref, mine_ref, other_ref, out_ref):
    core = core_ref[0]
    out_ref[pl.ds(core * SLOTS, SLOTS)] = mine_ref[...]
    out_ref[pl.ds((1 - core) * SLOTS, SLOTS)] = other_ref[...]


def join_call(core, mine, other):
    return pl.pallas_call(
        join_kernel,
        out_shape=jax.ShapeDtypeStruct((NC * SLOTS, SPAN, WIDTH), jnp.bfloat16),
        in_specs=[SMEM, VMEM, VMEM],
        out_specs=VMEM,
        compiler_params=pltpu.CompilerParams(vmem_limit_bytes=4 * 1024 * 1024),
        cost_estimate=pl.CostEstimate(flops=0, bytes_accessed=460_000, transcendentals=0),
        name="join",
    )(core, mine, other)


def along_z(values, k):
    index = [(z, core) for z in range(NZ) for core in range(NC)]
    pairs = [
        (z * NC + core, (z + (k if core == 0 else -k)) % NZ * NC + core) for z, core in index
    ]
    return lax.ppermute(values, ("z", "core"), pairs)


def shards(queries, stretch_kv, pool, owner, slot, enc_weight, dec_weight, cotangent):
    x, z, core = lax.axis_index("x"), lax.axis_index("z"), lax.axis_index("core")
    swap = [(0, 1), (1, 0)]

    own = lax.dynamic_slice_in_dim(dec_weight, core * HEAD_DIM, HEAD_DIM, axis=2)
    own = own.reshape(WIDTH, KV)
    enc_own = lax.dynamic_slice_in_dim(enc_weight, core * 384, 2 * KV, axis=1)
    packed = jnp.concatenate([own, enc_own[:, :KV], enc_own[:, KV:]], axis=0)
    packed = lax.all_gather(packed, ("core", "mp"), axis=0, tiled=False)

    qg = jnp.concatenate(
        [queries.reshape(NM, STRETCH, KV), cotangent.reshape(NM, STRETCH, KV)], axis=1
    )
    qg = lax.all_to_all(qg, "mp", split_axis=0, concat_axis=0, tiled=True)

    owner = owner.reshape(NX, NZ, NC, REQ)
    slot = slot.reshape(NX, NZ, NC, REQ)
    owner_core = owner % NC
    owner_z = (owner // NC) % NZ
    owner_x = owner // (NC * NZ)
    ahead = (owner_z - z) % NZ
    far = jnp.minimum(ahead, NZ - ahead)
    own_core = owner_core == core
    ask = (
        jnp.where(far == 0, 0, jnp.where(far == 4, 112, far * 32 - 16))
        + jnp.where((far > 0) & (ahead < 4), NC * SLOTS, 0)
        + owner_core * SLOTS
        + slot
    )
    back = jnp.where(core == 0, ahead < 4, ahead > 4) & (far > 0)
    place = slot + jnp.where(
        back,
        far * 2 * SLOTS - SLOTS + jnp.where(own_core, 0, SLOTS),
        jnp.where(own_core & (far == 0), 0, jnp.where(own_core & (far == 4), 56, NONE)),
    )
    place = jnp.where(owner_x == x, jnp.minimum(place, NONE), NONE)

    def of_column(values, which):
        return lax.dynamic_slice(values, (0, z, which, 0), (NX, 1, 1, REQ)).reshape(NX * REQ)

    beside = lax.ppermute(pool, "core", swap)
    chip = join_call(core.reshape(1).astype(jnp.int32), pool, beside)
    own_pool, _ = lax.optimization_barrier((pool, chip))
    came = [along_z(chip, k) for k in range(1, 4)] + [along_z(own_pool, 4)]
    parts = [chip] + [lax.all_gather(part, "core", axis=0, tiled=True) for part in came]
    ask = of_column(ask, core).reshape(NX, REQ)
    ask = jnp.take(ask, (x + jnp.arange(NX)) % NX, axis=0, mode="clip").reshape(NX * REQ)
    chosen = choose_call(ask, parts)
    arrived = [chosen[0]] + [
        lax.ppermute(chosen[k], "x", [(i, (i + k) % NX) for i in range(NX)]) for k in range(1, NX)
    ]
    my_x = lax.dynamic_slice(owner_x, (x, z, core, 0), (1, 1, 1, REQ)).reshape(REQ)
    (rows,) = choose_call((x - my_x) % NX * REQ + jnp.arange(REQ), arrived)
    rows, qg = lax.optimization_barrier((rows, qg))
    rows = lax.all_to_all(rows, "mp", split_axis=0, concat_axis=0, tiled=True)
    rows = rows.reshape(2 * STRETCH, WIDTH)
    _, packed = lax.optimization_barrier((chosen[0], packed))

    out, grad_rows = stretch_call(rows, stretch_kv, qg, packed)

    grad_rows = grad_rows.reshape(REQ, SPAN, WIDTH)
    grad_rows = lax.all_to_all(grad_rows, "mp", split_axis=0, concat_axis=0, tiled=True)
    every = lax.all_gather(grad_rows, "x", axis=0, tiled=True)
    every_beside = lax.ppermute(every, "core", swap)
    places = jnp.stack([of_column(place, core), of_column(place, 1 - core)])
    mine, *partial = place_call(places, every, every_beside)
    partial = [along_z(part, k) for k, part in enumerate(partial, 1)]
    out = lax.all_gather(out, "mp", axis=0, tiled=False)
    out = lax.dynamic_index_in_dim(out, lax.axis_index("mp"), 1, keepdims=False)
    attended = out[:, :STRETCH].reshape(NM * STRETCH, KV)
    grad_queries = out[:, STRETCH:].reshape(NM * STRETCH, KV)
    partial, attended, grad_queries = lax.optimization_barrier((partial, attended, grad_queries))
    partial = [part.astype(jnp.float32) for part in partial]
    ours = mine.astype(jnp.float32) + partial[3] + sum(part[:SLOTS] for part in partial[:3])
    theirs = sum(part[SLOTS:] for part in partial[:3]).astype(jnp.bfloat16)
    theirs = lax.all_gather(theirs, "core", axis=0, tiled=False)
    theirs = lax.dynamic_index_in_dim(theirs, 1 - core, 0, keepdims=False)
    grad_pool = ours + theirs.astype(jnp.float32)

    return attended, grad_queries, grad_pool


def solution(mesh):
    split = Mesh(mesh.devices.reshape(NX, NZ, NC, NM), ("x", "z", "core", "mp"))
    in_specs = (
        P(SEQ, "mp"),
        P(SEQ + ("mp",), None),
        P(SEQ, "mp", None),
        P(),
        P(),
        P("mp", None),
        P(None, None, "mp"),
        P(SEQ, "mp"),
    )
    out_specs = (P(SEQ, "mp"), P(SEQ, "mp"), P(SEQ, "mp", None))
    return jax.shard_map(shards, mesh=split, in_specs=in_specs, out_specs=out_specs, check_vma=False)
```

```python
import functools

import jax
import jax.numpy as jnp
from jax import lax
from jax.experimental import pallas as pl
from jax.experimental.pallas import tpu as pltpu
from jax.sharding import Mesh
from jax.sharding import PartitionSpec as P

HEAD_DIM = 128
SCALE = HEAD_DIM ** (-0.5)
SEQ = ("x", "z", "core")
NX, NZ, NC, NM = 4, 8, 2, 8
REQ = 16
SLOTS = 8
STRETCH = 64
SPAN = 8
WIDTH = 896
ENC_HEADS = 7
KV = 2 * HEAD_DIM
ENC_ROWS = 112
NONE = NZ * SLOTS


def dot(a, b, dims):
    return lax.dot_general(a, b, ((dims[0], dims[1]), ((), ())), preferred_element_type=jnp.float32)


def softmax(scores):
    top = jnp.max(scores, axis=-1, keepdims=True)
    e = jnp.exp(scores - top)
    return e * (1.0 / jnp.sum(e, axis=-1, keepdims=True))


def softmax_back(weights, grad):
    return weights * (grad - jnp.sum(grad * weights, axis=-1, keepdims=True))


def stretch_kernel(
    rows_ref,
    kv_ref,
    qg_ref,
    packed_ref,
    out_ref,
    grad_ref,
    enc_parts,
    enc_w,
    dec_w,
    encoded_ref,
    heads_ref,
    probs_ref,
    total_ref,
    enc_sem,
    dec_sem,
):
    enc_copy = pltpu.make_async_copy(
        packed_ref.at[:, pl.ds(WIDTH, 2 * ENC_ROWS), :], enc_parts, enc_sem
    )
    enc_copy.start()
    dec_copies = []
    for m in range(NM):
        group = []
        for core in range(NC):
            group.append(
                pltpu.make_async_copy(
                    packed_ref.at[core * NM + m, pl.ds(0, WIDTH), :],
                    dec_w.at[m, core],
                    dec_sem.at[m, core],
                )
            )
        dec_copies.append(group)
    enc_copy.wait()
    for group in dec_copies:
        for copy in group:
            copy.start()
    for m in range(NM):
        at = slice(m * ENC_ROWS, (m + 1) * ENC_ROWS)
        enc_w[at, :256] = enc_parts[m, :ENC_ROWS]
        enc_w[at, 256:512] = enc_parts[m, ENC_ROWS:]
        enc_w[at, 512:640] = enc_parts[NM + m, :ENC_ROWS, HEAD_DIM:]
        enc_w[at, 640:] = enc_parts[NM + m, ENC_ROWS:]

    rows = rows_ref[...]
    query = dot(rows, enc_w[...], ((1,), (0,))).astype(jnp.bfloat16)
    for h in range(ENC_HEADS):
        cols = slice(h * HEAD_DIM, (h + 1) * HEAD_DIM)
        keys = kv_ref[:, cols]
        values = kv_ref[:, WIDTH + h * HEAD_DIM : WIDTH + (h + 1) * HEAD_DIM]
        weights = softmax(dot(query[:, cols], keys, ((1,), (1,))) * SCALE)
        probs_ref[h] = weights
        mixed = dot(weights.astype(jnp.bfloat16), values, ((1,), (0,)))
        encoded_ref[:, cols] = (rows[:, cols].astype(jnp.float32) + mixed).astype(jnp.bfloat16)
    encoded = encoded_ref[...]

    left = lax.broadcasted_iota(jnp.int32, (STRETCH, KV), 1) < HEAD_DIM
    zero = jnp.zeros((STRETCH, KV), jnp.bfloat16)

    def stacked(pair):
        return jnp.concatenate([jnp.where(left, pair, zero), jnp.where(left, zero, pair)], axis=0)

    def beside(blocks):
        return jnp.where(left, blocks[:STRETCH], blocks[STRETCH:]).astype(jnp.bfloat16)

    for m in range(NM):
        for copy in dec_copies[m]:
            copy.wait()
        pair = [dot(encoded, dec_w[m, h], ((1,), (0,))).astype(jnp.bfloat16) for h in range(2)]
        keys = jnp.concatenate([both[:, :HEAD_DIM] for both in pair], axis=1)
        values = jnp.concatenate([both[:, HEAD_DIM:] for both in pair], axis=1)
        q = stacked(qg_ref[m, :STRETCH, :])
        g = stacked(qg_ref[m, STRETCH:, :])
        weights = softmax(dot(q, keys, ((1,), (1,))) * SCALE)
        low_w = weights.astype(jnp.bfloat16)
        out_ref[m, :STRETCH, :] = beside(dot(low_w, values, ((1,), (0,))))
        grad_s = softmax_back(weights, dot(g, values, ((1,), (1,)))).astype(jnp.bfloat16)
        out_ref[m, STRETCH:, :] = beside(dot(grad_s, keys, ((1,), (0,))) * SCALE)
        grad_v = dot(low_w, g, ((0,), (0,))).astype(jnp.bfloat16)
        grad_k = (dot(grad_s, q, ((0,), (0,))) * SCALE).astype(jnp.bfloat16)
        for h in range(2):
            cols = slice(h * HEAD_DIM, (h + 1) * HEAD_DIM)
            grads = jnp.concatenate([grad_k[:, cols], grad_v[:, cols]], axis=1)
            term = dot(grads, dec_w[m, h], ((1,), (1,)))
            if m == 0 and h == 0:
                total_ref[...] = term
            else:
                total_ref[...] += term

    grad_encoded = total_ref[...].astype(jnp.bfloat16)
    for h in range(ENC_HEADS):
        cols = slice(h * HEAD_DIM, (h + 1) * HEAD_DIM)
        keys = kv_ref[:, cols]
        values = kv_ref[:, WIDTH + h * HEAD_DIM : WIDTH + (h + 1) * HEAD_DIM]
        grad_w = dot(grad_encoded[:, cols], values, ((1,), (1,)))
        grad_s = softmax_back(probs_ref[h], grad_w).astype(jnp.bfloat16)
        heads_ref[:, cols] = (dot(grad_s, keys, ((1,), (0,))) * SCALE).astype(jnp.bfloat16)
    back = dot(heads_ref[...], enc_w[...], ((1,), (1,)))
    grad_ref[...] = (grad_encoded.astype(jnp.float32) + back).astype(jnp.bfloat16)


VMEM = pl.BlockSpec(memory_space=pltpu.VMEM)
SMEM = pl.BlockSpec(memory_space=pltpu.SMEM)


def stretch_call(rows, kv, qg, packed):
    return pl.pallas_call(
        stretch_kernel,
        out_shape=(
            jax.ShapeDtypeStruct((NM, 2 * STRETCH, KV), jnp.bfloat16),
            jax.ShapeDtypeStruct((2 * STRETCH, WIDTH), jnp.bfloat16),
        ),
        in_specs=[VMEM, VMEM, VMEM, pl.BlockSpec(memory_space=pltpu.HBM)],
        out_specs=(VMEM, VMEM),
        scratch_shapes=[
            pltpu.VMEM((NC * NM, 2 * ENC_ROWS, KV), jnp.bfloat16),
            pltpu.VMEM((WIDTH, WIDTH), jnp.bfloat16),
            pltpu.VMEM((NM, NC, WIDTH, KV), jnp.bfloat16),
            pltpu.VMEM((2 * STRETCH, WIDTH), jnp.bfloat16),
            pltpu.VMEM((2 * STRETCH, WIDTH), jnp.bfloat16),
            pltpu.VMEM((ENC_HEADS, 2 * STRETCH, STRETCH), jnp.float32),
            pltpu.VMEM((2 * STRETCH, WIDTH), jnp.float32),
            pltpu.SemaphoreType.DMA,
            pltpu.SemaphoreType.DMA((NM, NC)),
        ],
        compiler_params=pltpu.CompilerParams(vmem_limit_bytes=52 * 1024 * 1024),
        cost_estimate=pl.CostEstimate(
            flops=7_000_000_000, bytes_accessed=11_000_000, transcendentals=200_000
        ),
        name="stretch",
    )(rows, kv, qg, packed)


def choose_kernel(count, ask_ref, *refs):
    parts, out_refs, all_ref = refs[:count], refs[count:-1], refs[-1]
    at = 0
    for part in parts:
        all_ref[at : at + part.shape[0]] = part[...]
        at += part.shape[0]
    for number, out_ref in enumerate(out_refs):

        def copy(i, carry, number=number, out_ref=out_ref):
            out_ref[i] = all_ref[ask_ref[number * REQ + i]]
            return carry

        lax.fori_loop(0, REQ, copy, 0, unroll=8)


def choose_call(ask, parts):
    outs = ask.shape[0] // REQ
    total = sum(part.shape[0] for part in parts)
    return pl.pallas_call(
        functools.partial(choose_kernel, len(parts)),
        out_shape=(jax.ShapeDtypeStruct((REQ, SPAN, WIDTH), jnp.bfloat16),) * outs,
        in_specs=[SMEM] + [VMEM] * len(parts),
        out_specs=(VMEM,) * outs,
        scratch_shapes=[pltpu.VMEM((total, SPAN, WIDTH), jnp.bfloat16)],
        compiler_params=pltpu.CompilerParams(vmem_limit_bytes=12 * 1024 * 1024),
        cost_estimate=pl.CostEstimate(flops=0, bytes_accessed=3_000_000, transcendentals=0),
        name="choose",
    )(ask, *parts)


def place_kernel(place_ref, mine_ref, other_ref, *refs):
    *out_refs, total_ref = refs
    total_ref[...] = jnp.zeros_like(total_ref)
    for source, ref in enumerate((mine_ref, other_ref)):

        def add(i, carry, ref=ref, source=source):
            at = place_ref[source, i]
            total_ref[at] += ref[i].astype(jnp.float32)
            return carry

        lax.fori_loop(0, NX * REQ, add, 0, unroll=8)
    at = 0
    for ref in out_refs:
        ref[...] = total_ref[at : at + ref.shape[0]].astype(jnp.bfloat16)
        at += ref.shape[0]


def place_call(place, mine, other):
    return pl.pallas_call(
        place_kernel,
        out_shape=tuple(
            jax.ShapeDtypeStruct((count * SLOTS, SPAN, WIDTH), jnp.bfloat16)
            for count in (1, 2, 2, 2, 1)
        ),
        in_specs=[SMEM, VMEM, VMEM],
        out_specs=(VMEM,) * 5,
        scratch_shapes=[pltpu.VMEM((NONE + 1, SPAN, WIDTH), jnp.float32)],
        compiler_params=pltpu.CompilerParams(vmem_limit_bytes=12 * 1024 * 1024),
        cost_estimate=pl.CostEstimate(
            flops=1_000_000, bytes_accessed=3_000_000, transcendentals=0
        ),
        name="place",
    )(place, mine, other)


def join_kernel(core_ref, mine_ref, other_ref, out_ref):
    core = core_ref[0]
    out_ref[pl.ds(core * SLOTS, SLOTS)] = mine_ref[...]
    out_ref[pl.ds((1 - core) * SLOTS, SLOTS)] = other_ref[...]


def join_call(core, mine, other):
    return pl.pallas_call(
        join_kernel,
        out_shape=jax.ShapeDtypeStruct((NC * SLOTS, SPAN, WIDTH), jnp.bfloat16),
        in_specs=[SMEM, VMEM, VMEM],
        out_specs=VMEM,
        compiler_params=pltpu.CompilerParams(vmem_limit_bytes=4 * 1024 * 1024),
        cost_estimate=pl.CostEstimate(flops=0, bytes_accessed=460_000, transcendentals=0),
        name="join",
    )(core, mine, other)


def along_z(values, k):
    index = [(z, core) for z in range(NZ) for core in range(NC)]
    pairs = [
        (z * NC + core, (z + (k if core == 0 else -k)) % NZ * NC + core) for z, core in index
    ]
    return lax.ppermute(values, ("z", "core"), pairs)


def shards(queries, stretch_kv, pool, owner, slot, enc_weight, dec_weight, cotangent):
    x, z, core = lax.axis_index("x"), lax.axis_index("z"), lax.axis_index("core")
    swap = [(0, 1), (1, 0)]

    own = lax.dynamic_slice_in_dim(dec_weight, core * HEAD_DIM, HEAD_DIM, axis=2)
    own = own.reshape(WIDTH, KV)
    enc_own = lax.dynamic_slice_in_dim(enc_weight, core * 384, 2 * KV, axis=1)
    packed = jnp.concatenate([own, enc_own[:, :KV], enc_own[:, KV:]], axis=0)
    packed = lax.all_gather(packed, ("core", "mp"), axis=0, tiled=False)

    qg = jnp.concatenate(
        [queries.reshape(NM, STRETCH, KV), cotangent.reshape(NM, STRETCH, KV)], axis=1
    )
    qg = lax.all_to_all(qg, "mp", split_axis=0, concat_axis=0, tiled=True)

    owner = owner.reshape(NX, NZ, NC, REQ)
    slot = slot.reshape(NX, NZ, NC, REQ)
    owner_core = owner % NC
    owner_z = (owner // NC) % NZ
    owner_x = owner // (NC * NZ)
    ahead = (owner_z - z) % NZ
    far = jnp.minimum(ahead, NZ - ahead)
    own_core = owner_core == core
    ask = (
        jnp.where(far == 0, 0, jnp.where(far == 4, 112, far * 32 - 16))
        + jnp.where((far > 0) & (ahead < 4), NC * SLOTS, 0)
        + owner_core * SLOTS
        + slot
    )
    back = jnp.where(core == 0, ahead < 4, ahead > 4) & (far > 0)
    place = slot + jnp.where(
        back,
        far * 2 * SLOTS - SLOTS + jnp.where(own_core, 0, SLOTS),
        jnp.where(own_core & (far == 0), 0, jnp.where(own_core & (far == 4), 56, NONE)),
    )
    place = jnp.where(owner_x == x, jnp.minimum(place, NONE), NONE)

    def of_column(values, which):
        return lax.dynamic_slice(values, (0, z, which, 0), (NX, 1, 1, REQ)).reshape(NX * REQ)

    beside = lax.ppermute(pool, "core", swap)
    chip = join_call(core.reshape(1).astype(jnp.int32), pool, beside)
    own_pool, _ = lax.optimization_barrier((pool, chip))
    came = [along_z(chip, k) for k in range(1, 4)] + [along_z(own_pool, 4)]
    parts = [chip] + [lax.all_gather(part, "core", axis=0, tiled=True) for part in came]
    ask = of_column(ask, core).reshape(NX, REQ)
    ask = jnp.take(ask, (x + jnp.arange(NX)) % NX, axis=0, mode="clip").reshape(NX * REQ)
    chosen = choose_call(ask, parts)
    arrived = [chosen[0]] + [
        lax.ppermute(chosen[k], "x", [(i, (i + k) % NX) for i in range(NX)]) for k in range(1, NX)
    ]
    my_x = lax.dynamic_slice(owner_x, (x, z, core, 0), (1, 1, 1, REQ)).reshape(REQ)
    step = ((x - my_x) % NX)[:, None, None]
    rows = jnp.where(
        step < 2,
        jnp.where(step == 0, arrived[0], arrived[1]),
        jnp.where(step == 2, arrived[2], arrived[3]),
    )
    rows, qg = lax.optimization_barrier((rows, qg))
    rows = lax.all_to_all(rows, "mp", split_axis=0, concat_axis=0, tiled=True)
    rows = rows.reshape(2 * STRETCH, WIDTH)
    _, packed = lax.optimization_barrier((chosen[0], packed))

    out, grad_rows = stretch_call(rows, stretch_kv, qg, packed)

    grad_rows = grad_rows.reshape(REQ, SPAN, WIDTH)
    grad_rows = lax.all_to_all(grad_rows, "mp", split_axis=0, concat_axis=0, tiled=True)
    every = lax.all_gather(grad_rows, "x", axis=0, tiled=True)
    every_beside = lax.ppermute(every, "core", swap)
    places = jnp.stack([of_column(place, core), of_column(place, 1 - core)])
    mine, *partial = place_call(places, every, every_beside)
    partial = [along_z(part, k) for k, part in enumerate(partial, 1)]
    out = lax.all_gather(out, "mp", axis=0, tiled=False)
    out = lax.dynamic_index_in_dim(out, lax.axis_index("mp"), 1, keepdims=False)
    attended = out[:, :STRETCH].reshape(NM * STRETCH, KV)
    grad_queries = out[:, STRETCH:].reshape(NM * STRETCH, KV)
    partial, attended, grad_queries = lax.optimization_barrier((partial, attended, grad_queries))
    partial = [part.astype(jnp.float32) for part in partial]
    ours = mine.astype(jnp.float32) + partial[3] + sum(part[:SLOTS] for part in partial[:3])
    theirs = sum(part[SLOTS:] for part in partial[:3]).astype(jnp.bfloat16)
    theirs = lax.all_gather(theirs, "core", axis=0, tiled=False)
    theirs = lax.dynamic_index_in_dim(theirs, 1 - core, 0, keepdims=False)
    grad_pool = ours + theirs.astype(jnp.float32)

    return attended, grad_queries, grad_pool


def solution(mesh):
    split = Mesh(mesh.devices.reshape(NX, NZ, NC, NM), ("x", "z", "core", "mp"))
    in_specs = (
        P(SEQ, "mp"),
        P(SEQ + ("mp",), None),
        P(SEQ, "mp", None),
        P(),
        P(),
        P("mp", None),
        P(None, None, "mp"),
        P(SEQ, "mp"),
    )
    out_specs = (P(SEQ, "mp"), P(SEQ, "mp"), P(SEQ, "mp", None))
    return jax.shard_map(shards, mesh=split, in_specs=in_specs, out_specs=out_specs, check_vma=False)
```
